32 devices in a mesh: ctx: 2 (over y), ep: 16 (over z, x, core).
Axes of the slice: x: 2, y: 2, z: 4, core: 2. Of those that a mesh axis runs over, the one named last changes fastest.
Arguments:
- queries: bfloat16 [256, 73728], P('ctx', 'ep'), may hold values from -12 to 12
- latent: bfloat16 [256, 576], P('ctx'), may hold values from -5 to 5
- doc_ids: int32 [256], replicated, may hold values from 0 to 3, never falling along the last dimension, each value on 1 to 128 neighbouring positions
- w_uv: bfloat16 [128, 512, 128], P('ep'), may hold values from -0.75 to 0.75
- w_out: bfloat16 [16384, 7168], P('ep', 'ctx'), may hold values from -0.046875 to 0.046875
- hidden_in: bfloat16 [256, 7168], P('ep', 'ctx'), may hold values from -24 to 24
- norm_gain: float32 [7168], P('ctx'), may hold values from 0.5 to 1.5
- route_ids: int32 [256, 8], P('ep'), may hold values from 0 to 15, all different within a row; in each aligned block of 16 rows (0 to 15, 16 to 31, ...) at most 9 rows name the same one
- route_weights: float32 [256, 8], P('ep'), may hold values from 0.1 to 1
- w_gate: bfloat16 [16, 7168, 1024], P('ep', 'ctx'), may hold values from -0.0625 to 0.0625
- w_up: bfloat16 [16, 7168, 1024], P('ep', 'ctx'), may hold values from -0.0625 to 0.0625
- w_down: bfloat16 [16, 1024, 7168], P('ep', None, 'ctx'), may hold values from -0.1875 to 0.1875
Outputs:
- layer_output: bfloat16 [256, 7168], P('ep', 'ctx')
The draws below stay inside these ranges and needn't reach their ends.
Inputs may be any that keep to these rules, and one draw needn't show every extreme that they name: `doc_ids`: document numbers never fall along the sequence; a document has at most 128 tokens, and one has exactly that many. `route_ids`: each token names 8 different experts; among the 16 tokens of one index of ep no expert is named by more than 9 tokens, a bound that some block reaches.
All inputs are finite; a program needn't handle non-finite values.
Results may differ from the reference program's by a relative error of at most 0.014.
Values may be sent and summed in bfloat16 or wider, within the bound.
No kernel may reach another device: no remote copies, remote signals or barrier semaphores. Data moves between devices by JAX's collectives and lax.ppermute only.
A program may use at most 64 MiB of HBM per device.

```python
import math
import jax
import jax.numpy as jnp
import numpy as np
from jax import lax

D = 7168
HEADS = 128
KVL = 512
ROPE = 64
VDIM = 128
FF = 1024
TOP = 8
EXPERTS = 16
L = 256
TOKD = 16
HEADS_DEV = 8
CAP = 9
N_CTX = 2
N_EP = 16


def attention_inputs(key):
    width = KVL + ROPE
    base_key = jax.random.fold_in(key, 4242)
    first, second = jax.random.split(base_key, 2)
    keys_out = jnp.clip(jax.random.normal(first, (L, width), jnp.float32), -4.0, 4.0)
    query_out = 0.5 * jnp.clip(jax.random.normal(second, (L, HEADS, width), jnp.float32), -4.0, 4.0)
    return (query_out.reshape(L, HEADS * width), keys_out)


def draw_queries(key, part):
    return attention_inputs(key)[0].astype(jnp.bfloat16)


def draw_latent(key, part):
    return attention_inputs(key)[1].astype(jnp.bfloat16)


def draw_hidden_in(key, part):
    first = jax.random.fold_in(jax.random.fold_in(key, 77), 0)
    columns = jnp.exp(math.log(3.0) * jnp.arange(D, dtype=jnp.float32) / (D - 1))
    values = jnp.clip(jax.random.normal(first, (L, D), jnp.float32), -4.0, 4.0)
    return (values * columns[None, :]).astype(jnp.bfloat16)


def level_of(stream_key, shape, shards, smallest, high):
    factor_of = 1.0
    for position, shards_of in shards:
        draws = jax.random.uniform(jax.random.fold_in(jax.random.fold_in(stream_key, 6), position), (shards_of,), jnp.float32, smallest / len(shards), high / len(shards))
        factor_of = factor_of * jnp.repeat(jnp.exp(draws), shape[position] // shards_of).reshape((-1,) + (1,) * (len(shape) - 1 - position))
    return factor_of


def profile(count, total, reach, slope):
    portions = [(1 << 20) // math.isqrt(standing ** slope) + 1 for standing in range(2, count + 1)]
    surplus, counts = total - reach - (count - 1), [1] * (count - 1)
    while surplus > 0:
        free = [i for i in range(count - 1) if counts[i] < reach]
        mass, left = sum([portions[i] for i in free]), surplus
        for i in free:
            extra = min(reach - counts[i], max(1, left * portions[i] // mass), surplus)
            counts[i] = counts[i] + extra
            surplus = surplus - extra
    return np.array([reach] + counts)


def ragged(rng, number_of, total, bound, slope):
    if number_of == 2:
        one = jax.random.randint(rng, (), max(1, total - bound), min(bound, total - 1) + 1)
        return jnp.stack([one, total - one])
    tallies = jnp.asarray(profile(number_of, total, bound, slope), jnp.int32)
    couples = (number_of - 1) // 2
    donor, taker = tallies[1:1 + 2 * couples:2], tallies[2:2 + 2 * couples:2]
    slack = jnp.minimum(donor - 1, bound - taker)
    passed = jax.random.randint(jax.random.fold_in(rng, 1), (couples,), 0, 1 << 20) % (slack + 1)
    tallies = tallies.at[1:1 + 2 * couples:2].set(donor - passed).at[2:2 + 2 * couples:2].set(taker + passed)
    return tallies[jax.random.permutation(jax.random.fold_in(rng, 2), number_of)]


def routed_block(rng, own, number, rows, amount, top, limit, slope):
    sequence = jax.random.permutation(rng, amount)
    packed, usual = shares(amount, rows * top, limit, slope, True), shares(amount, rows * top, limit, slope, False)
    places = jnp.arange(amount)

    def named(sizes, turn):
        used = int((sizes > 0).sum())
        fixed = max(1, used // 4)
        moved = fixed + (places - fixed + turn * (used - fixed)) % max(1, amount - fixed)
        return jnp.zeros((amount,), jnp.int32).at[sequence[jnp.where(places < fixed, places, moved)]].set(jnp.asarray(sizes, jnp.int32))

    sizes = jnp.where(number % 4 == 0, named(packed, number // 4), named(usual, number - number // 4 - 1))
    mixed = jax.random.permutation(jax.random.fold_in(own, 3), amount)
    donor, receiver = mixed[0:amount // 2 * 2:2], mixed[1:amount // 2 * 2:2]
    room = jnp.minimum(sizes[donor] - 1, limit - sizes[receiver]) // 2
    room = jnp.where((donor == sequence[0]) | (receiver == sequence[0]) | (sizes[receiver] == 0), 0, jnp.maximum(room, 0))
    moved = jax.random.randint(jax.random.fold_in(own, 4), (amount // 2,), 0, 1 << 20) % (room + 1)
    sizes = sizes.at[donor].add(-moved).at[receiver].add(moved)
    members = jnp.searchsorted(jnp.cumsum(sizes), jnp.arange(rows * top), side="right").astype(jnp.int32)
    grid = members.reshape(top, rows).T
    grid = grid[jax.random.permutation(jax.random.fold_in(own, 1), rows)]
    turn = jax.random.randint(jax.random.fold_in(own, 2), (rows, 1), 0, top)
    return jnp.take_along_axis(grid, (jnp.arange(top)[None, :] + turn) % top, axis=1)


def shares(number_of, total, reach, skew, full):
    portions = [(1 << 20) // math.isqrt(rank ** skew) + 1 for rank in range(1, number_of + 1)]
    largest = reach if full else min(reach, max(-(-total // number_of), total * portions[0] // sum(portions)))
    least = 1 if total - largest >= number_of - 1 else 0
    holding, rest = [largest] + [least] * (number_of - 1), total - largest - least * (number_of - 1)
    while rest > 0:
        free = [i for i in range(1, number_of) if holding[i] < largest] or [i for i in range(1, number_of) if holding[i] < reach]
        mass, remaining = sum([portions[i] for i in free]), rest
        for i in free:
            addition = min(reach - holding[i], max(1, remaining * portions[i] // mass), rest)
            holding[i] = holding[i] + addition
            rest = rest - addition
    return np.array(holding)


def bell_draw(key, shape, deviation, limit, cuts=(), kind=jnp.bfloat16):
    values = jax.random.normal(key, shape, jnp.float32) * deviation
    if len(cuts) > 0:
        values = level_of(key, shape, cuts, -0.22, 0.18) * values
    return jnp.clip(values, min=-limit, max=limit).astype(kind)


def setup_inputs(seed: int = 0) -> dict:
    key_list = jax.random.split(jax.random.key(seed), 13)
    queries = draw_queries(jax.random.fold_in(key_list[12], 71), 0)
    latent = draw_latent(jax.random.fold_in(key_list[12], 71), 0)
    doc_ids = jnp.searchsorted(jnp.cumsum(ragged(key_list[2], 4, L, L // 2, 1)), jnp.arange(L), side="right").astype(jnp.int32)
    w_uv = bell_draw(key_list[3], (HEADS, KVL, VDIM), (KVL // 9) ** -0.5, 0.75, ((0, 16),))
    w_out = bell_draw(key_list[4], (HEADS * VDIM, D), (HEADS * VDIM) ** -0.5, 0.046875, ((0, 16), (1, 2)))
    hidden_in = draw_hidden_in(jax.random.fold_in(key_list[12], 71), 0)
    norm_gain = jnp.clip(1.0 + 0.1 * jax.random.normal(key_list[6], (D,), jnp.float32), 0.5, 1.5)
    route_ids_keys = jax.random.split(jax.random.fold_in(key_list[7], 1), L // TOKD)
    route_ids_turns = jax.random.permutation(jax.random.fold_in(key_list[7], 3), L // TOKD)
    route_ids = jax.vmap(lambda own, number: routed_block(jax.random.fold_in(key_list[7], 2), own, number, TOKD, EXPERTS, TOP, CAP, 2))(route_ids_keys, route_ids_turns).reshape((L, TOP))
    route_weights = jnp.clip(jnp.exp(math.log(1.0) - 2.3025851 * jax.random.uniform(key_list[8], (L, TOP), jnp.float32) ** level_of(key_list[8], (L, TOP), ((0, 16),), -0.2, 0.2)), 0.1, 1.0)
    w_gate = bell_draw(key_list[9], (EXPERTS, D, FF), D ** -0.5, 0.0625, ((0, 16), (1, 2)))
    w_up = bell_draw(key_list[10], (EXPERTS, D, FF), D ** -0.5, 0.0625, ((0, 16), (1, 2)))
    w_down = bell_draw(key_list[11], (EXPERTS, FF, D), FF ** -0.5, 0.1875, ((0, 16), (2, 2)))
    return {"queries": queries, "latent": latent, "doc_ids": doc_ids, "w_uv": w_uv, "w_out": w_out, "hidden_in": hidden_in, "norm_gain": norm_gain, "route_ids": route_ids, "route_weights": route_weights, "w_gate": w_gate, "w_up": w_up, "w_down": w_down}


score_scale = (1.0 + 0.1 * math.log(40.0)) ** 2 / math.sqrt(192.0)
masked_score = -1e+30

def reference(queries, latent, doc_ids, w_uv, w_out, hidden_in, norm_gain, route_ids, route_weights, w_gate, w_up, w_down):
    key_width = KVL + ROPE
    positions = jnp.arange(L, dtype=jnp.int32)
    allowed = (positions[None, :] <= positions[:, None]) & (doc_ids[None, :] == doc_ids[:, None])
    latent_full = latent.astype(jnp.float32)
    values_full = latent_full[:, :KVL]

    def one_group(running, group):
        start = (group * HEADS_DEV * key_width).astype(jnp.int32)
        block = lax.dynamic_slice_in_dim(queries, start, HEADS_DEV * key_width, 1)
        block = block.reshape(L, HEADS_DEV, key_width).astype(jnp.float32)
        scores = jnp.einsum('qhc,kc->hqk', block, latent_full) * score_scale
        scores = jnp.where(allowed[None], scores, masked_score)
        peak = lax.optimization_barrier(jnp.max(scores, axis=2, keepdims=True))
        probs = jnp.where(allowed[None], jnp.exp(scores - peak), 0.0)
        totals = lax.optimization_barrier(jnp.sum(probs, axis=2))
        rounded = lax.optimization_barrier(probs.astype(jnp.bfloat16)).astype(jnp.float32)
        context = (jnp.einsum('hqk,kc->hqc', rounded, values_full) / totals[:, :, None]).astype(jnp.bfloat16)
        head_start = (group * HEADS_DEV).astype(jnp.int32)
        up_weights = lax.dynamic_slice_in_dim(w_uv, head_start, HEADS_DEV, 0).astype(jnp.float32)
        head_values = jnp.einsum('hqc,hcv->qhv', context.astype(jnp.float32), up_weights)
        head_values = head_values.reshape(L, HEADS_DEV * VDIM).astype(jnp.bfloat16)
        row_start = (group * HEADS_DEV * VDIM).astype(jnp.int32)
        out_rows = lax.dynamic_slice_in_dim(w_out, row_start, HEADS_DEV * VDIM, 0)
        partial_value = jnp.dot(head_values, out_rows, preferred_element_type=jnp.float32)
        partial_value = lax.optimization_barrier(partial_value.astype(jnp.bfloat16)).astype(jnp.float32)
        return (running + partial_value, 0)
    attended, unused = lax.scan(one_group, jnp.zeros((L, D), jnp.float32), jnp.arange(N_EP, dtype=jnp.int32))
    residual = hidden_in.astype(jnp.float32) + attended
    normed = residual * lax.rsqrt(lax.optimization_barrier(jnp.mean(residual * residual, axis=1, keepdims=True)) + 1e-06) * norm_gain
    normed = normed.astype(jnp.bfloat16)
    pair_ids = route_ids.reshape(N_EP, TOKD * TOP)
    chosen = (pair_ids[:, :, None] == jnp.arange(EXPERTS, dtype=jnp.int32)[None, None, :]).astype(jnp.int32)
    earlier = jnp.cumsum(chosen, axis=1) - chosen
    slot = lax.optimization_barrier(jnp.sum(earlier * chosen, axis=2))
    sources = jnp.arange(N_EP, dtype=jnp.int32)[:, None]
    where_to = (pair_ids * (N_EP * CAP) + sources * CAP + slot).reshape(-1).astype(jnp.int32)
    owners = (jnp.arange(L * TOP, dtype=jnp.int32) // TOP).astype(jnp.int32)
    table = jnp.full((EXPERTS * N_EP * CAP,), L, jnp.int32).at[where_to].set(owners)
    padded = jnp.concatenate([normed, jnp.zeros((1, D), jnp.bfloat16)], axis=0)

    def one_expert(pieces):
        index, gate_weight, up_weight, down_weight = pieces
        taken = padded[index].reshape(N_EP * CAP, N_CTX, D // N_CTX).astype(jnp.float32)
        gate_parts = jnp.einsum('mcd,cdf->cmf', taken, gate_weight.reshape(N_CTX, D // N_CTX, FF).astype(jnp.float32))
        up_parts = jnp.einsum('mcd,cdf->cmf', taken, up_weight.reshape(N_CTX, D // N_CTX, FF).astype(jnp.float32))
        gate = lax.optimization_barrier(jnp.sum(lax.optimization_barrier(gate_parts.astype(jnp.bfloat16)).astype(jnp.float32), axis=0))
        upper = lax.optimization_barrier(jnp.sum(lax.optimization_barrier(up_parts.astype(jnp.bfloat16)).astype(jnp.float32), axis=0))
        activated = (jax.nn.silu(gate) * upper).astype(jnp.bfloat16)
        return jnp.dot(activated, down_weight, preferred_element_type=jnp.float32).astype(jnp.bfloat16)
    outputs = lax.map(one_expert, (table.reshape(EXPERTS, N_EP * CAP), w_gate, w_up, w_down))
    returned = outputs.reshape(EXPERTS * N_EP * CAP, D)[where_to]
    mixture = lax.optimization_barrier(jnp.sum(returned.astype(jnp.float32).reshape(L, TOP, D) * route_weights[:, :, None], axis=1))
    return (residual + mixture).astype(jnp.bfloat16)
```

```python
import math

import jax
import jax.numpy as jnp
from jax import lax
from jax.sharding import PartitionSpec as P

D = 7168
KVL = 512


score_scale = (1.0 + 0.1 * math.log(40.0)) ** 2 / math.sqrt(192.0)
masked_score = -1e30
EXTRA = 128


def pairs(count, bit):
    return [(index, index ^ (1 << bit)) for index in range(count)]


def split_columns(array, parts):
    lanes = array.shape[-1] // 128
    edges = [lanes * part // parts * 128 for part in range(parts)] + [array.shape[-1]]
    return [array[..., low:high] for low, high in zip(edges[:-1], edges[1:]) if high > low]


def orders_of(bits):
    straight = list(range(bits))
    turned = [0] + straight[2:] + straight[1:2]
    return [straight, turned]


def opened(array, bits, bit):
    place = bits.index(bit)
    low, high = 1 << place, 1 << (len(bits) - 1 - place)
    return array.reshape((high, 2, low) + array.shape[1:])


def scatter_sum(parts, orders, count):
    bits = len(orders[0])
    states = [(part, list(range(bits))) for part in parts]
    for step in range(bits):
        following = []
        for (array, left), order in zip(states, orders):
            bit = order[step]
            both = opened(array, left, bit)
            shape = (-1,) + array.shape[1:]
            kept = both[:, 0].reshape(shape)
            got = lax.ppermute(both[:, 1].reshape(shape), "ep", pairs(count, bit))
            total = kept.astype(jnp.float32) + got.astype(jnp.float32)
            if step < bits - 1:
                total = total.astype(jnp.bfloat16)
            following.append((total, [other for other in left if other != bit]))
        states = following
    return jnp.concatenate([array[0] for array, left in states], axis=-1)


def gather_chunks(parts, orders, count):
    states = [(part[None], []) for part in parts]
    for step in range(len(orders[0])):
        following = []
        for (array, held), order in zip(states, orders):
            bit = order[-1 - step]
            got = lax.ppermute(array, "ep", pairs(count, bit))
            now = sorted(held + [bit])
            place = now.index(bit)
            low, high = 1 << place, 1 << (len(now) - 1 - place)
            shape = (high, low) + array.shape[1:]
            joined = jnp.stack([array.reshape(shape), got.reshape(shape)], axis=1)
            following.append((joined.reshape((-1,) + array.shape[1:]), now))
        states = following
    return [array for array, held in states]


def attend(heads_local, query_first, keys, key_first, doc_ids):
    count = heads_local.shape[0]
    key_count = keys.shape[0]
    scores = (
        jnp.einsum("nhc,kc->hnk", heads_local, keys, preferred_element_type=jnp.float32)
        * score_scale
    )
    query_pos = query_first + jnp.arange(count, dtype=jnp.int32)
    key_pos = key_first + jnp.arange(key_count, dtype=jnp.int32)
    query_doc = lax.dynamic_slice_in_dim(doc_ids, query_first, count)
    key_doc = jnp.sum(
        jnp.where(
            key_pos[:, None] == jnp.arange(doc_ids.shape[0], dtype=jnp.int32)[None, :],
            doc_ids[None, :] + 1,
            0,
        ),
        axis=1,
    )
    allowed = (key_pos[None, :] <= query_pos[:, None]) & (
        key_doc[None, :] == query_doc[:, None] + 1
    )
    scores = jnp.where(allowed[None], scores, masked_score)
    peak = jnp.max(scores, axis=2)
    probs = jnp.where(allowed[None], jnp.exp(scores - peak[:, :, None]), 0.0)
    total = jnp.sum(probs, axis=2)
    context = jnp.einsum(
        "hnk,kc->hnc",
        probs.astype(jnp.bfloat16),
        keys[:, :KVL],
        preferred_element_type=jnp.float32,
    )
    return (context / total[:, :, None]).astype(jnp.bfloat16)


def three_terms(values):
    first = values.astype(jnp.bfloat16)
    rest = values - first.astype(jnp.float32)
    second = rest.astype(jnp.bfloat16)
    third = (rest - second.astype(jnp.float32)).astype(jnp.bfloat16)
    return first, second, third


def shards(
    queries,
    latent,
    doc_ids,
    w_uv,
    w_out,
    hidden_in,
    norm_gain,
    route_ids,
    route_weights,
    w_gate,
    w_up,
    w_down,
):
    ctx_count = lax.axis_size("ctx")
    ep_count = lax.axis_size("ep")
    ctx_rank = lax.axis_index("ctx")
    ep_rank = lax.axis_index("ep")
    bits = ep_count.bit_length() - 1
    orders = orders_of(bits)
    block_rows = queries.shape[0]
    head_count = w_uv.shape[0]
    key_width = latent.shape[1]
    token_count = hidden_in.shape[0]
    top_count = route_ids.shape[1]
    all_tokens = ep_count * token_count
    heads_local = queries.reshape(block_rows, head_count, key_width)
    own_first = ctx_rank * block_rows
    swap = [(0, 1), (1, 0)]

    if ctx_count == 2:
        earlier_keys = lax.ppermute(latent, "ctx", [(0, 1)])
        keys = jnp.concatenate([earlier_keys, latent], axis=0)
        key_first = own_first - block_rows
    else:
        keys = lax.all_gather(latent, "ctx", axis=0, tiled=True)
        key_first = jnp.int32(0)
    context = attend(heads_local, own_first, keys, key_first, doc_ids)
    head_values = jnp.einsum("hnc,hcv->nhv", context, w_uv, preferred_element_type=jnp.float32)
    head_values = head_values.reshape(block_rows, -1).astype(jnp.bfloat16)

    chunk = jnp.arange(all_tokens, dtype=jnp.int32) // token_count
    source = ep_rank ^ chunk
    if ctx_count == 2:
        other = lax.ppermute(head_values, "ctx", swap)
        all_values = jnp.concatenate([head_values, other], axis=0)
        per_block = ep_count // 2
        source = source % per_block + per_block * (source // per_block != ctx_rank)
    else:
        all_values = lax.all_gather(head_values, "ctx", axis=0, tiled=True)
    row = source * token_count + jnp.arange(all_tokens, dtype=jnp.int32) % token_count
    ordering = (row[:, None] == jnp.arange(all_tokens, dtype=jnp.int32)[None, :]).astype(
        jnp.bfloat16
    )
    all_values = jnp.dot(ordering, all_values, preferred_element_type=jnp.float32).astype(
        jnp.bfloat16
    )
    partial_parts = [
        jnp.dot(all_values, part, preferred_element_type=jnp.float32)
        .astype(jnp.bfloat16)
        .reshape(ep_count, token_count, -1)
        for part in split_columns(w_out, len(orders))
    ]
    attended = scatter_sum(partial_parts, orders, ep_count)
    residual = hidden_in.astype(jnp.float32) + attended

    squares = jnp.sum(residual * residual, axis=1)
    gained = (residual * norm_gain).astype(jnp.bfloat16)
    experts = jnp.arange(ep_count, dtype=jnp.int32)
    named = route_ids[:, :, None] == experts[None, None, :]
    chosen = jnp.sum(named.astype(jnp.float32), axis=1)
    weights = jnp.sum(jnp.where(named, route_weights[:, :, None], 0.0), axis=1)
    token_index = jnp.arange(token_count, dtype=jnp.int32)
    before = (token_index[:, None] > token_index[None, :]).astype(jnp.float32)
    place = jnp.sum(before[:, :, None] * chosen[None, :, :], axis=1)
    place = jnp.where(chosen > 0, place, -1.0).astype(jnp.bfloat16)
    extra = [place, *three_terms(weights), *(term[:, None] for term in three_terms(squares))]
    extra_width = sum(part.shape[1] for part in extra)
    padded = -(-extra_width // EXTRA) * EXTRA
    extra.append(jnp.zeros((token_count, padded - extra_width), jnp.bfloat16))
    sent = split_columns(jnp.concatenate([gained, *extra], axis=1), len(orders))
    arrived = jnp.concatenate(gather_chunks(sent, orders, ep_count), axis=2)
    arrived = arrived.reshape(all_tokens, -1)
    width = gained.shape[1]
    features = arrived[:, :width]
    facts = arrived[:, width:].astype(jnp.float32)

    capacity = min(token_count, max(2, token_count * top_count * 9 // (8 * ep_count)))
    slots = ep_count * capacity
    mine = (experts == ep_rank).astype(jnp.float32)
    of_expert = [
        jnp.sum(facts[:, part * ep_count : (part + 1) * ep_count] * mine[None, :], axis=1)
        for part in range(4)
    ]
    token_place = of_expert[0].astype(jnp.int32)
    token_weight = of_expert[1] + of_expert[2] + of_expert[3]
    token_squares = jnp.sum(facts[:, 4 * ep_count : 4 * ep_count + 3], axis=1)
    if ctx_count == 2:
        token_squares = token_squares + lax.ppermute(token_squares, "ctx", swap)
    else:
        token_squares = lax.psum(token_squares, "ctx")
    token_scale = lax.rsqrt(token_squares / D + 1e-06)
    token_slot = jnp.where(token_place >= 0, chunk * capacity + token_place, -1)
    placing = jnp.arange(slots, dtype=jnp.int32)[:, None] == token_slot[None, :]
    slot_scale = jnp.sum(jnp.where(placing, token_scale[None, :], 0.0), axis=1)
    slot_weight = jnp.sum(jnp.where(placing, token_weight[None, :], 0.0), axis=1)
    placing = placing.astype(jnp.bfloat16)
    rows = jnp.dot(placing, features, preferred_element_type=jnp.float32).astype(jnp.bfloat16)
    both = jnp.concatenate(
        [
            jnp.dot(rows, w_gate[0], preferred_element_type=jnp.float32).astype(jnp.bfloat16),
            jnp.dot(rows, w_up[0], preferred_element_type=jnp.float32).astype(jnp.bfloat16),
        ],
        axis=1,
    )
    if ctx_count == 2:
        both = both.astype(jnp.float32) + lax.ppermute(both, "ctx", swap).astype(jnp.float32)
    else:
        both = lax.psum(both, "ctx").astype(jnp.float32)
    both = both * slot_scale[:, None]
    hidden = both.shape[1] // 2
    activated = (jax.nn.silu(both[:, :hidden]) * both[:, hidden:]).astype(jnp.bfloat16)
    returned = []
    for part in split_columns(w_down[0], len(orders)):
        produced = jnp.dot(activated, part, preferred_element_type=jnp.float32)
        produced = (produced * slot_weight[:, None]).astype(jnp.bfloat16)
        spread = lax.dot_general(
            placing, produced, (((0,), (0,)), ((), ())), preferred_element_type=jnp.float32
        )
        returned.append(spread.astype(jnp.bfloat16).reshape(ep_count, token_count, -1))
    mixture = scatter_sum(returned, orders, ep_count)
    return (residual + mixture).astype(jnp.bfloat16)


def solution(mesh):
    return jax.shard_map(
        shards,
        mesh=mesh,
        in_specs=(
            P("ctx", "ep"),
            P("ctx", None),
            P(),
            P("ep", None, None),
            P("ep", "ctx"),
            P("ep", "ctx"),
            P("ctx"),
            P("ep", None),
            P("ep", None),
            P("ep", "ctx", None),
            P("ep", "ctx", None),
            P("ep", None, "ctx"),
        ),
        out_specs=P("ep", "ctx"),
        check_vma=False,
    )
```

```python
import functools
import math

import jax
import jax.numpy as jnp
from jax import lax
from jax.experimental import pallas as pl
from jax.experimental.pallas import tpu as pltpu
from jax.sharding import PartitionSpec as P

D = 7168
KVL = 512


score_scale = (1.0 + 0.1 * math.log(40.0)) ** 2 / math.sqrt(192.0)
masked_score = -1e30
PARTS = 2


def split_edges(width, parts):
    lanes = width // 128
    edges = [lanes * part // parts * 128 for part in range(parts)] + [width]
    return [(low, high) for low, high in zip(edges[:-1], edges[1:]) if high > low]


def split_columns(array, parts):
    return [array[..., low:high] for low, high in split_edges(array.shape[-1], parts)]


def step_bits(bits, lane):
    middle = list(range(1, bits - 1))
    if lane:
        middle = middle[1:] + middle[:1]
    return [0] + middle + [bits - 1]


def crossing(count, step):
    bits = count.bit_length() - 1
    return [(index, index ^ (1 << step_bits(bits, index & 1)[step])) for index in range(count)]


def chunk_owners(count, rank):
    bits = count.bit_length() - 1
    number = jnp.arange(count, dtype=jnp.int32)
    flip = number >> (bits - 1)
    distances = []
    for lane in range(2):
        order = step_bits(bits, lane)
        distance = jnp.zeros((count,), jnp.int32)
        for step in range(1, bits):
            distance = distance | ((number >> (bits - 1 - step)) & 1) << order[step]
        distances.append(distance)
    other_lane = ((rank & 1) ^ flip) == 1
    return rank ^ flip ^ jnp.where(other_lane, distances[1], distances[0])


def halved(array, step, count):
    half = array.shape[0] // 2
    got = lax.ppermute(array[half:], "ep", crossing(count, step))
    return array[:half].astype(jnp.float32) + got.astype(jnp.float32)


def doubled(array, step, count):
    return jnp.concatenate([array, lax.ppermute(array, "ep", crossing(count, step))], axis=0)


def scores_kernel(pair_count, query_ref, keys_ref, heads_ref, scores_ref):
    rows = query_ref.shape[0]
    pair_width = query_ref.shape[1] // pair_count
    width = heads_ref.shape[1]
    half = pair_count * rows
    for side in range(2):
        first = side * (pair_width - width)
        for pair in range(pair_count):
            at = side * half + pair * rows
            low = pair * pair_width + first
            heads_ref[at : at + rows, :] = query_ref[:, low : low + width]
        part = slice(side * half, (side + 1) * half)
        scores_ref[part, :] = jnp.dot(
            heads_ref[part, :], padded_keys(keys_ref, width, side), preferred_element_type=jnp.float32
        )


def padded_keys(keys_ref, width, side):
    zeros = jnp.zeros((width - keys_ref.shape[0], keys_ref.shape[1]), jnp.bfloat16)
    parts = [zeros, keys_ref[...]] if side else [keys_ref[...], zeros]
    return jnp.concatenate(parts, axis=0)


def attend_kernel(pair_count, doc_ref, heads_ref, scores_ref, up_ref, *refs):
    blocks, out_ref = refs[:-1], refs[-1]
    rows = out_ref.shape[0]
    half = pair_count * rows
    width = heads_ref.shape[1]
    value_width = up_ref.shape[2]
    rank = lax.axis_index("ctx")

    def docs_of(first, count):
        return doc_ref[:, pl.ds(pl.multiple_of(first, 128), count)]

    own_first = rank * rows
    query_doc = jnp.broadcast_to(docs_of(own_first, rows), (rows, rows)).T[:, 0:1]
    firsts = [jnp.int32(0)] if len(blocks) == 1 else [own_first, (1 - rank) * rows]
    scores, masks = [], []
    for first, block in zip(firsts, blocks):
        count = block.shape[1]
        key_pos = first + lax.broadcasted_iota(jnp.int32, (rows, count), 1)
        query_pos = own_first + lax.broadcasted_iota(jnp.int32, (rows, count), 0)
        allowed = (key_pos <= query_pos) & (docs_of(first, count) == query_doc)
        masks.append(jnp.where(allowed, 1.0, 0.0))
        if block is blocks[0]:
            scores.append(scores_ref[...])
        else:
            sides = [
                jnp.dot(
                    heads_ref[side * half : (side + 1) * half, :],
                    padded_keys(block, width, side),
                    preferred_element_type=jnp.float32,
                )
                for side in range(2)
            ]
            scores.append(jnp.concatenate(sides, axis=0))
    allowed = jnp.concatenate([jnp.concatenate(masks, axis=1)] * (2 * pair_count), axis=0) > 0
    scores = jnp.where(allowed, jnp.concatenate(scores, axis=1) * score_scale, masked_score)
    peak = jnp.max(scores, axis=1, keepdims=True)
    probs = jnp.where(allowed, jnp.exp(scores - peak), 0.0)
    total = jnp.sum(probs, axis=1, keepdims=True)
    context = lax.dot_general(
        probs.astype(jnp.bfloat16),
        jnp.concatenate([block[:KVL, :] for block in blocks], axis=1),
        (((1,), (1,)), ((), ())),
        preferred_element_type=jnp.float32,
    )
    context = (context / total).astype(jnp.bfloat16)
    for pair in range(pair_count):
        for side in range(2):
            at = side * half + pair * rows
            head = 2 * pair + side
            out_ref[:, head * value_width : (head + 1) * value_width] = jnp.dot(
                context[at : at + rows], up_ref[head], preferred_element_type=jnp.float32
            ).astype(jnp.bfloat16)


def whole_block(shape):
    return pl.BlockSpec(shape, lambda step: (0,) * len(shape))


def attend(queries, blocks, doc_ids, w_uv):
    rows = queries.shape[0]
    head_count, value_in, value_width = w_uv.shape
    query_width = queries.shape[1] // head_count
    key_count = doc_ids.shape[0]
    width = -(-query_width // 128) * 128
    pair_count = 2 if head_count % 4 == 0 and key_count <= 512 else 1
    heads = 2 * pair_count
    grid = (head_count // heads,)
    first_keys = blocks[0].shape[1]
    params = pltpu.CompilerParams(
        vmem_limit_bytes=(8 << 20) + 8 * heads * rows * (key_count + KVL) * 4
    )
    stacked = lambda columns: pl.BlockSpec((heads * rows, columns), lambda step: (step, 0))
    arranged, scores = pl.pallas_call(
        functools.partial(scores_kernel, pair_count),
        out_shape=(
            jax.ShapeDtypeStruct((head_count * rows, width), jnp.bfloat16),
            jax.ShapeDtypeStruct((head_count * rows, first_keys), jnp.float32),
        ),
        grid=grid,
        in_specs=[
            pl.BlockSpec((rows, heads * query_width), lambda step: (0, step)),
            whole_block(blocks[0].shape),
        ],
        out_specs=(stacked(width), stacked(first_keys)),
        compiler_params=params,
        cost_estimate=pl.CostEstimate(
            flops=2 * rows * head_count * first_keys * width,
            bytes_accessed=2 * queries.size,
            transcendentals=0,
        ),
        name="first_scores",
    )(queries, blocks[0])
    return pl.pallas_call(
        functools.partial(attend_kernel, pair_count),
        out_shape=jax.ShapeDtypeStruct((rows, head_count * value_width), jnp.bfloat16),
        grid=grid,
        in_specs=[
            whole_block((1, key_count)),
            stacked(width),
            stacked(first_keys),
            pl.BlockSpec((heads, value_in, value_width), lambda step: (step, 0, 0)),
            *(whole_block(block.shape) for block in blocks),
        ],
        out_specs=pl.BlockSpec((rows, heads * value_width), lambda step: (0, step)),
        compiler_params=params,
        cost_estimate=pl.CostEstimate(
            flops=2 * rows * head_count * key_count * (query_width + value_in),
            bytes_accessed=2 * (queries.size + w_uv.size),
            transcendentals=rows * head_count * key_count,
        ),
        name="attention",
    )(doc_ids[None], arranged, scores, w_uv, *blocks)


def fetch_kernel(pieces, first, from_ref, after_ref, to_ref, sems):
    rows = from_ref.shape[0] // pieces
    columns = pl.ds(first, to_ref.shape[1])
    copies = []
    for piece in range(pieces):
        part = pl.ds(piece * rows, rows)
        copies.append(
            pltpu.make_async_copy(
                from_ref.at[part, columns], to_ref.at[part], sems.at[piece]
            )
        )
    for copy in copies:
        copy.start()
    for copy in copies:
        copy.wait()


def fetched(weights, after, edges=None):
    pieces = 4
    low, high = edges or (0, weights.shape[1])
    return pl.pallas_call(
        functools.partial(fetch_kernel, pieces, low),
        out_shape=pltpu.VMEM((weights.shape[0], high - low), weights.dtype),
        in_specs=[
            pl.BlockSpec(memory_space=pltpu.HBM),
            pl.BlockSpec(memory_space=pl.ANY),
        ],
        out_specs=pl.BlockSpec(memory_space=pltpu.VMEM),
        scratch_shapes=[pltpu.SemaphoreType.DMA((pieces,))],
        compiler_params=pltpu.CompilerParams(vmem_limit_bytes=1 << 20),
        cost_estimate=pl.CostEstimate(
            flops=0, bytes_accessed=2 * weights.shape[0] * (high - low) * weights.dtype.itemsize, transcendentals=0
        ),
        name="fetch_weights",
    )(weights, after)


def norm_part(own_ref, got_ref, gain_ref, kept_ref, sent_ref):
    width = own_ref.shape[2]
    squares = []
    for chunk in range(2):
        residual = own_ref[chunk] + got_ref[1 - chunk, :, :width].astype(jnp.float32)
        if chunk == 0:
            kept_ref[...] = residual
        sent_ref[chunk, :, :width] = (residual * gain_ref[...]).astype(jnp.bfloat16)
        squares.append(jnp.sum(residual * residual, axis=1, keepdims=True))
    return squares


def first_norm_kernel(own_ref, got_ref, gain_ref, kept_ref, sent_ref, squares_ref):
    for chunk, squares in enumerate(norm_part(own_ref, got_ref, gain_ref, kept_ref, sent_ref)):
        squares_ref[chunk] = squares


def last_norm_kernel(
    facts_width, own_ref, got_ref, gain_ref, squares_ref, facts_ref, kept_ref, sent_ref
):
    width = own_ref.shape[2]
    for chunk, squares in enumerate(norm_part(own_ref, got_ref, gain_ref, kept_ref, sent_ref)):
        facts = facts_ref[...] if chunk == 0 else got_ref[0, :, width:]
        facts = facts.astype(jnp.float32)
        lane = lax.broadcasted_iota(jnp.int32, facts.shape, 1)
        for place, term in enumerate(three_terms(squares + squares_ref[chunk])):
            facts = jnp.where(lane == facts_width + place, term.astype(jnp.float32), facts)
        sent_ref[chunk, :, width:] = facts.astype(jnp.bfloat16)


def normalised(facts_width, own, got, gain, squares=None, facts=None):
    rows, width = own.shape[1:]
    vmem = pl.BlockSpec(memory_space=pltpu.VMEM)
    if squares is None:
        return pl.pallas_call(
            first_norm_kernel,
            out_shape=(
                jax.ShapeDtypeStruct((rows, width), jnp.float32),
                jax.ShapeDtypeStruct((2, rows, width), jnp.bfloat16),
                jax.ShapeDtypeStruct((2, rows, 1), jnp.float32),
            ),
            in_specs=[vmem] * 3,
            out_specs=(vmem,) * 3,
            compiler_params=pltpu.CompilerParams(vmem_limit_bytes=4 << 20),
            name="norm",
        )(own, got, gain[None])
    return pl.pallas_call(
        functools.partial(last_norm_kernel, facts_width),
        out_shape=(
            jax.ShapeDtypeStruct((rows, width), jnp.float32),
            jax.ShapeDtypeStruct((2, rows, width + facts.shape[1]), jnp.bfloat16),
        ),
        in_specs=[vmem] * 5,
        out_specs=(vmem,) * 2,
        compiler_params=pltpu.CompilerParams(vmem_limit_bytes=4 << 20),
        name="norm_last",
    )(own, got, gain[None], squares, facts)


def three_terms(values):
    first = values.astype(jnp.bfloat16)
    rest = values - first.astype(jnp.float32)
    second = rest.astype(jnp.bfloat16)
    third = (rest - second.astype(jnp.float32)).astype(jnp.bfloat16)
    return first, second, third


def shards(
    queries,
    latent,
    doc_ids,
    w_uv,
    w_out,
    hidden_in,
    norm_gain,
    route_ids,
    route_weights,
    w_gate,
    w_up,
    w_down,
):
    ctx_count = lax.axis_size("ctx")
    ep_count = lax.axis_size("ep")
    ctx_rank = lax.axis_index("ctx")
    ep_rank = lax.axis_index("ep")
    bits = ep_count.bit_length() - 1
    block_rows = queries.shape[0]
    token_count = hidden_in.shape[0]
    top_count = route_ids.shape[1]
    all_tokens = ep_count * token_count
    swap = [(0, 1), (1, 0)]

    key_columns = latent.T
    if ctx_count == 2:
        blocks = [key_columns, lax.ppermute(key_columns, "ctx", [(0, 1)])]
    else:
        blocks = [lax.all_gather(key_columns, "ctx", axis=1, tiled=True)]
    head_values = attend(queries, blocks, doc_ids, w_uv)
    route_ids, route_weights, head_values = lax.optimization_barrier(
        (route_ids, route_weights, head_values)
    )

    owner = jnp.repeat(chunk_owners(ep_count, ep_rank), token_count)
    chunk = jnp.arange(all_tokens, dtype=jnp.int32) // token_count
    if ctx_count == 2:
        other = lax.ppermute(head_values, "ctx", swap)
        w_out = fetched(w_out, head_values)
        all_values = jnp.concatenate([head_values, other], axis=0)
        per_block = ep_count // 2
        owner = owner % per_block + per_block * (owner // per_block != ctx_rank)
    else:
        all_values = lax.all_gather(head_values, "ctx", axis=0, tiled=True)
    row = owner * token_count + jnp.arange(all_tokens, dtype=jnp.int32) % token_count
    ordering = (row[:, None] == jnp.arange(all_tokens, dtype=jnp.int32)[None, :]).astype(
        jnp.bfloat16
    )
    all_values = jnp.dot(ordering, all_values, preferred_element_type=jnp.float32).astype(
        jnp.bfloat16
    )

    experts = jnp.arange(ep_count, dtype=jnp.int32)
    named = route_ids[:, :, None] == experts[None, None, :]
    chosen = jnp.sum(named.astype(jnp.float32), axis=1)
    weights = jnp.sum(jnp.where(named, route_weights[:, :, None], 0.0), axis=1)
    token_index = jnp.arange(token_count, dtype=jnp.int32)
    before = (token_index[:, None] > token_index[None, :]).astype(jnp.float32)
    place = jnp.sum(before[:, :, None] * chosen[None, :, :], axis=1)
    place = jnp.where(chosen > 0, place, -1.0).astype(jnp.bfloat16)
    facts = jnp.concatenate([place, *three_terms(weights)], axis=1)
    facts_width = facts.shape[1]
    padded = -(-(facts_width + 3) // 128) * 128
    facts = jnp.pad(facts, ((0, 0), (0, padded - facts_width)))

    edges = split_edges(w_out.shape[1], PARTS)
    residuals, arrived = [], []
    squares = jnp.zeros((2, token_count, 1), jnp.float32)
    for part, (low, high) in enumerate(edges):
        array = (
            jnp.dot(all_values, w_out[:, low:high], preferred_element_type=jnp.float32)
            .astype(jnp.bfloat16)
            .reshape(ep_count, token_count, -1)
        )
        for step in range(bits - 1):
            total = halved(array, step, ep_count)
            array = total.astype(jnp.bfloat16)
        own = total[0] + hidden_in[:, low:high].astype(jnp.float32)
        total = jnp.stack([own, total[1]])
        sent = total.astype(jnp.bfloat16)
        last = part == len(edges) - 1
        if last:
            sent = jnp.concatenate([sent, jnp.stack([facts, jnp.zeros_like(facts)])], axis=2)
        got = lax.ppermute(sent, "ep", crossing(ep_count, bits - 1))
        if part == 0:
            gate_weights = fetched(w_gate[0], sent)
            up_weights = fetched(w_up[0], sent)
        width = high - low
        if last:
            kept, array = normalised(facts_width, total, got, norm_gain[low:high], squares, facts)
        else:
            kept, array, more = normalised(facts_width, total, got, norm_gain[low:high])
            squares = squares + more
        residuals.append(kept)
        for step in range(bits - 2, -1, -1):
            array = doubled(array, step, ep_count)
        arrived.append(array.reshape(all_tokens, -1))
    facts = arrived[-1][:, width:].astype(jnp.float32)
    arrived[-1] = arrived[-1][:, :width]

    capacity = min(token_count, max(2, token_count * top_count * 9 // (8 * ep_count)))
    slots = ep_count * capacity
    mine = (experts == ep_rank).astype(jnp.float32)
    of_expert = [
        jnp.sum(facts[:, part * ep_count : (part + 1) * ep_count] * mine[None, :], axis=1)
        for part in range(4)
    ]
    token_place = of_expert[0].astype(jnp.int32)
    token_weight = of_expert[1] + of_expert[2] + of_expert[3]
    token_squares = jnp.sum(facts[:, 4 * ep_count : 4 * ep_count + 3], axis=1)
    if ctx_count == 2:
        token_squares = token_squares + lax.ppermute(token_squares, "ctx", swap)
    else:
        token_squares = lax.psum(token_squares, "ctx")
    token_scale = lax.rsqrt(token_squares / D + 1e-06)
    token_slot = jnp.where(token_place >= 0, chunk * capacity + token_place, -1)
    placing = jnp.arange(slots, dtype=jnp.int32)[:, None] == token_slot[None, :]
    slot_scale = jnp.sum(jnp.where(placing, token_scale[None, :], 0.0), axis=1)
    slot_weight = jnp.sum(jnp.where(placing, token_weight[None, :], 0.0), axis=1)
    placing = placing.astype(jnp.bfloat16)
    both = 0.0
    for (low, high), features in zip(edges, arrived):
        rows = jnp.dot(placing, features, preferred_element_type=jnp.float32).astype(jnp.bfloat16)
        both = both + jnp.concatenate(
            [
                jnp.dot(rows, gate_weights[low:high], preferred_element_type=jnp.float32),
                jnp.dot(rows, up_weights[low:high], preferred_element_type=jnp.float32),
            ],
            axis=1,
        )
    both = both.astype(jnp.bfloat16)
    if ctx_count == 2:
        down_weights = fetched(w_down[0], both)
        other_both = lax.ppermute(both, "ctx", swap)
        both = both.astype(jnp.float32) + other_both.astype(jnp.float32)
    else:
        down_weights = w_down[0]
        both = lax.psum(both, "ctx").astype(jnp.float32)
    both = both * slot_scale[:, None]
    hidden = both.shape[1] // 2
    activated = (jax.nn.silu(both[:, :hidden]) * both[:, hidden:]).astype(jnp.bfloat16)
    spread = placing.T
    outputs = []
    for (low, high), residual in zip(edges, residuals):
        produced = jnp.dot(activated, down_weights[:, low:high], preferred_element_type=jnp.float32)
        produced = (produced * slot_weight[:, None]).astype(jnp.bfloat16)
        produced = lax.optimization_barrier(produced)
        array = (
            jnp.dot(spread, produced, preferred_element_type=jnp.float32)
            .astype(jnp.bfloat16)
            .reshape(ep_count, token_count, -1)
        )
        for step in range(bits):
            total = halved(array, step, ep_count)
            array = total.astype(jnp.bfloat16)
        outputs.append((residual + total[0]).astype(jnp.bfloat16))
    return jnp.concatenate(outputs, axis=1)


def solution(mesh):
    return jax.shard_map(
        shards,
        mesh=mesh,
        in_specs=(
            P("ctx", "ep"),
            P("ctx", None),
            P(),
            P("ep", None, None),
            P("ep", "ctx"),
            P("ep", "ctx"),
            P("ctx"),
            P("ep", None),
            P("ep", None),
            P("ep", "ctx", None),
            P("ep", "ctx", None),
            P("ep", None, "ctx"),
        ),
        out_specs=P("ep", "ctx"),
        check_vma=False,
    )
```

```python
import functools
import math

import jax
import jax.numpy as jnp
from jax import lax
from jax.experimental import pallas as pl
from jax.experimental.pallas import tpu as pltpu
from jax.sharding import PartitionSpec as P

D = 7168
KVL = 512


score_scale = (1.0 + 0.1 * math.log(40.0)) ** 2 / math.sqrt(192.0)
masked_score = -1e30
PARTS = 2
HIDDEN_PARTS = 2


def split_edges(width, parts):
    lanes = width // 128
    edges = [lanes * part // parts * 128 for part in range(parts)] + [width]
    return [(low, high) for low, high in zip(edges[:-1], edges[1:]) if high > low]


def split_columns(array, parts):
    return [array[..., low:high] for low, high in split_edges(array.shape[-1], parts)]


def step_bits(bits, lane):
    middle = list(range(1, bits - 1))
    if lane:
        middle = middle[1:] + middle[:1]
    return [0] + middle + [bits - 1]


def crossing(count, step):
    bits = count.bit_length() - 1
    return [(index, index ^ (1 << step_bits(bits, index & 1)[step])) for index in range(count)]


def chunk_owners(count, rank, lane, number):
    bits = count.bit_length() - 1
    flip = number >> (bits - 1)
    distances = []
    for side in range(2):
        order = step_bits(bits, side)
        distance = jnp.zeros_like(number)
        for step in range(1, bits):
            distance = distance | ((number >> (bits - 1 - step)) & 1) << order[step]
        distances.append(distance)
    other_lane = (lane ^ flip) == 1
    return rank ^ flip ^ jnp.where(other_lane, distances[1], distances[0])


def halved(array, step, count):
    half = array.shape[0] // 2
    got = lax.ppermute(array[half:], "ep", crossing(count, step))
    return array[:half].astype(jnp.float32) + got.astype(jnp.float32)


def doubled(array, step, count):
    return jnp.concatenate([array, lax.ppermute(array, "ep", crossing(count, step))], axis=0)


def scores_kernel(
    pair_count,
    query_ref,
    keys_ref,
    up_ref,
    doc_ref,
    heads_ref,
    scores_ref,
    own_ref,
    up_out_ref,
    doc_out_ref,
):
    own_ref[...] = keys_ref[...]
    up_out_ref[...] = up_ref[...]
    doc_out_ref[...] = doc_ref[...]
    rows = query_ref.shape[0]
    pair_width = query_ref.shape[1] // pair_count
    width = heads_ref.shape[1]
    half = pair_count * rows
    for side in range(2):
        first = side * (pair_width - width)
        for pair in range(pair_count):
            at = side * half + pair * rows
            low = pair * pair_width + first
            heads_ref[at : at + rows, :] = query_ref[:, low : low + width]
        part = slice(side * half, (side + 1) * half)
        scores_ref[part, :] = jnp.dot(
            heads_ref[part, :], padded_keys(keys_ref, width, side), preferred_element_type=jnp.float32
        )


def padded_keys(keys_ref, width, side):
    zeros = jnp.zeros((width - keys_ref.shape[0], keys_ref.shape[1]), jnp.bfloat16)
    parts = [zeros, keys_ref[...]] if side else [keys_ref[...], zeros]
    return jnp.concatenate(parts, axis=0)


def attend_kernel(pair_count, doc_ref, heads_ref, scores_ref, up_ref, *refs):
    blocks, out_ref = refs[:-1], refs[-1]
    rows = out_ref.shape[0]
    half = pair_count * rows
    width = heads_ref.shape[1]
    value_width = up_ref.shape[2]
    rank = lax.axis_index("ctx")

    def docs_of(first, count):
        return doc_ref[:, pl.ds(pl.multiple_of(first, 128), count)]

    own_first = rank * rows
    query_doc = jnp.broadcast_to(docs_of(own_first, rows), (rows, rows)).T[:, 0:1]
    firsts = [jnp.int32(0)] if len(blocks) == 1 else [own_first, (1 - rank) * rows]
    scores, masks = [], []
    for first, block in zip(firsts, blocks):
        count = block.shape[1]
        key_pos = first + lax.broadcasted_iota(jnp.int32, (rows, count), 1)
        query_pos = own_first + lax.broadcasted_iota(jnp.int32, (rows, count), 0)
        allowed = (key_pos <= query_pos) & (docs_of(first, count) == query_doc)
        masks.append(jnp.where(allowed, 1.0, 0.0))
        if block is blocks[0]:
            scores.append(scores_ref[...])
        else:
            sides = [
                jnp.dot(
                    heads_ref[side * half : (side + 1) * half, :],
                    padded_keys(block, width, side),
                    preferred_element_type=jnp.float32,
                )
                for side in range(2)
            ]
            scores.append(jnp.concatenate(sides, axis=0))
    allowed = jnp.concatenate([jnp.concatenate(masks, axis=1)] * (2 * pair_count), axis=0) > 0
    scores = jnp.where(allowed, jnp.concatenate(scores, axis=1) * score_scale, masked_score)
    peak = jnp.max(scores, axis=1, keepdims=True)
    probs = jnp.where(allowed, jnp.exp(scores - peak), 0.0)
    total = jnp.sum(probs, axis=1, keepdims=True)
    context = lax.dot_general(
        probs.astype(jnp.bfloat16),
        jnp.concatenate([block[:KVL, :] for block in blocks], axis=1),
        (((1,), (1,)), ((), ())),
        preferred_element_type=jnp.float32,
    )
    context = (context / total).astype(jnp.bfloat16)
    for pair in range(pair_count):
        for side in range(2):
            at = side * half + pair * rows
            head = 2 * pair + side
            out_ref[:, head * value_width : (head + 1) * value_width] = jnp.dot(
                context[at : at + rows], up_ref[head], preferred_element_type=jnp.float32
            ).astype(jnp.bfloat16)


def whole_block(shape):
    return pl.BlockSpec(shape, lambda step: (0,) * len(shape))


def attend(queries, blocks, doc_ids, w_uv):
    rows = queries.shape[0]
    head_count, value_in, value_width = w_uv.shape
    query_width = queries.shape[1] // head_count
    key_count = doc_ids.shape[0]
    width = -(-query_width // 128) * 128
    pair_count = 2 if head_count % 4 == 0 and key_count <= 512 else 1
    heads = 2 * pair_count
    grid = (head_count // heads,)
    first_keys = blocks[0].shape[1]
    params = pltpu.CompilerParams(
        vmem_limit_bytes=(8 << 20) + 8 * heads * rows * (key_count + KVL) * 4
    )
    stacked = lambda columns: pl.BlockSpec((heads * rows, columns), lambda step: (step, 0))
    up_block = pl.BlockSpec((heads, value_in, value_width), lambda step: (step, 0, 0))
    arranged, scores, own, w_uv, docs = pl.pallas_call(
        functools.partial(scores_kernel, pair_count),
        out_shape=(
            jax.ShapeDtypeStruct((head_count * rows, width), jnp.bfloat16),
            jax.ShapeDtypeStruct((head_count * rows, first_keys), jnp.float32),
            jax.ShapeDtypeStruct(blocks[0].shape, jnp.bfloat16),
            jax.ShapeDtypeStruct(w_uv.shape, jnp.bfloat16),
            jax.ShapeDtypeStruct((1, key_count), jnp.int32),
        ),
        grid=grid,
        in_specs=[
            pl.BlockSpec((rows, heads * query_width), lambda step: (0, step)),
            whole_block(blocks[0].shape),
            up_block,
            whole_block((1, key_count)),
        ],
        out_specs=(
            stacked(width),
            stacked(first_keys),
            whole_block(blocks[0].shape),
            up_block,
            whole_block((1, key_count)),
        ),
        compiler_params=params,
        cost_estimate=pl.CostEstimate(
            flops=2 * rows * head_count * first_keys * width,
            bytes_accessed=2 * queries.size,
            transcendentals=0,
        ),
        name="first_scores",
    )(queries, blocks[0], w_uv, doc_ids[None])
    return pl.pallas_call(
        functools.partial(attend_kernel, pair_count),
        out_shape=jax.ShapeDtypeStruct((rows, head_count * value_width), jnp.bfloat16),
        grid=grid,
        in_specs=[
            whole_block((1, key_count)),
            stacked(width),
            stacked(first_keys),
            up_block,
            *(whole_block(block.shape) for block in blocks),
        ],
        out_specs=pl.BlockSpec((rows, heads * value_width), lambda step: (0, step)),
        compiler_params=params,
        cost_estimate=pl.CostEstimate(
            flops=2 * rows * head_count * key_count * (query_width + value_in),
            bytes_accessed=2 * (queries.size + w_uv.size),
            transcendentals=rows * head_count * key_count,
        ),
        name="attention",
    )(docs, arranged, scores, w_uv, own, *blocks[1:])


def fetch_kernel(pieces, first, from_ref, after_ref, to_ref, sems):
    rows = from_ref.shape[0] // pieces
    columns = pl.ds(first, to_ref.shape[1])
    copies = []
    for piece in range(pieces):
        part = pl.ds(piece * rows, rows)
        copies.append(
            pltpu.make_async_copy(
                from_ref.at[part, columns], to_ref.at[part], sems.at[piece]
            )
        )
    for copy in copies:
        copy.start()
    for copy in copies:
        copy.wait()


def fetched(weights, after, edges=None):
    pieces = 4
    low, high = edges or (0, weights.shape[1])
    return pl.pallas_call(
        functools.partial(fetch_kernel, pieces, low),
        out_shape=pltpu.VMEM((weights.shape[0], high - low), weights.dtype),
        in_specs=[
            pl.BlockSpec(memory_space=pltpu.HBM),
            pl.BlockSpec(memory_space=pl.ANY),
        ],
        out_specs=pl.BlockSpec(memory_space=pltpu.VMEM),
        scratch_shapes=[pltpu.SemaphoreType.DMA((pieces,))],
        compiler_params=pltpu.CompilerParams(vmem_limit_bytes=1 << 20),
        cost_estimate=pl.CostEstimate(
            flops=0, bytes_accessed=2 * weights.shape[0] * (high - low) * weights.dtype.itemsize, transcendentals=0
        ),
        name="fetch_weights",
    )(weights, after)


def norm_part(own_ref, got_ref, gain_ref, kept_ref, sent_ref):
    width = own_ref.shape[2]
    squares = []
    for chunk in range(2):
        residual = own_ref[chunk] + got_ref[1 - chunk, :, :width].astype(jnp.float32)
        if chunk == 0:
            kept_ref[...] = residual
        sent_ref[chunk, :, :width] = (residual * gain_ref[...]).astype(jnp.bfloat16)
        squares.append(jnp.sum(residual * residual, axis=1, keepdims=True))
    return squares


def first_norm_kernel(own_ref, got_ref, gain_ref, kept_ref, sent_ref, squares_ref):
    for chunk, squares in enumerate(norm_part(own_ref, got_ref, gain_ref, kept_ref, sent_ref)):
        squares_ref[chunk] = squares


def last_norm_kernel(
    facts_width, own_ref, got_ref, gain_ref, squares_ref, facts_ref, kept_ref, sent_ref
):
    width = own_ref.shape[2]
    for chunk, squares in enumerate(norm_part(own_ref, got_ref, gain_ref, kept_ref, sent_ref)):
        facts = facts_ref[...] if chunk == 0 else got_ref[0, :, width:]
        facts = facts.astype(jnp.float32)
        lane = lax.broadcasted_iota(jnp.int32, facts.shape, 1)
        for place, term in enumerate(three_terms(squares + squares_ref[chunk])):
            facts = jnp.where(lane == facts_width + place, term.astype(jnp.float32), facts)
        sent_ref[chunk, :, width:] = facts.astype(jnp.bfloat16)


def normalised(facts_width, own, got, gain, squares=None, facts=None):
    rows, width = own.shape[1:]
    vmem = pl.BlockSpec(memory_space=pltpu.VMEM)
    if squares is None:
        return pl.pallas_call(
            first_norm_kernel,
            out_shape=(
                jax.ShapeDtypeStruct((rows, width), jnp.float32),
                jax.ShapeDtypeStruct((2, rows, width), jnp.bfloat16),
                jax.ShapeDtypeStruct((2, rows, 1), jnp.float32),
            ),
            in_specs=[vmem] * 3,
            out_specs=(vmem,) * 3,
            compiler_params=pltpu.CompilerParams(vmem_limit_bytes=4 << 20),
            name="norm",
        )(own, got, gain[None])
    return pl.pallas_call(
        functools.partial(last_norm_kernel, facts_width),
        out_shape=(
            jax.ShapeDtypeStruct((rows, width), jnp.float32),
            jax.ShapeDtypeStruct((2, rows, width + facts.shape[1]), jnp.bfloat16),
        ),
        in_specs=[vmem] * 5,
        out_specs=(vmem,) * 2,
        compiler_params=pltpu.CompilerParams(vmem_limit_bytes=4 << 20),
        name="norm_last",
    )(own, got, gain[None], squares, facts)


def three_terms(values):
    first = values.astype(jnp.bfloat16)
    rest = values - first.astype(jnp.float32)
    second = rest.astype(jnp.bfloat16)
    third = (rest - second.astype(jnp.float32)).astype(jnp.bfloat16)
    return first, second, third


def shards(
    queries,
    latent,
    doc_ids,
    w_uv,
    w_out,
    hidden_in,
    norm_gain,
    route_ids,
    route_weights,
    w_gate,
    w_up,
    w_down,
):
    ctx_count = lax.axis_size("ctx")
    ep_count = lax.axis_size("ep")
    ctx_rank = lax.axis_index("ctx")
    ep_rank = lax.axis_index("ep")
    bits = ep_count.bit_length() - 1
    block_rows = queries.shape[0]
    token_count = hidden_in.shape[0]
    top_count = route_ids.shape[1]
    all_tokens = ep_count * token_count
    swap = [(0, 1), (1, 0)]

    key_columns, ctx_rank, ep_rank, lane = lax.optimization_barrier(
        (latent.T, ctx_rank, ep_rank, ep_rank & 1)
    )
    if ctx_count == 2:
        blocks = [key_columns, lax.ppermute(key_columns, "ctx", [(0, 1)])]
    else:
        blocks = [lax.all_gather(key_columns, "ctx", axis=1, tiled=True)]
    head_values = attend(queries, blocks, doc_ids, w_uv)
    route_ids, route_weights, norm_gain, head_values = lax.optimization_barrier(
        (route_ids, route_weights, norm_gain, head_values)
    )

    chunk = jnp.arange(all_tokens, dtype=jnp.int32) // token_count
    owner = chunk_owners(ep_count, ep_rank, lane, chunk)
    if ctx_count == 2:
        other = lax.ppermute(head_values, "ctx", swap)
        w_out = fetched(w_out, head_values)
        all_values = jnp.concatenate([head_values, other], axis=0)
        per_block = ep_count // 2
        owner = owner % per_block + per_block * (owner // per_block != ctx_rank)
    else:
        all_values = lax.all_gather(head_values, "ctx", axis=0, tiled=True)
    row = owner * token_count + jnp.arange(all_tokens, dtype=jnp.int32) % token_count
    ordering = (row[:, None] == jnp.arange(all_tokens, dtype=jnp.int32)[None, :]).astype(
        jnp.bfloat16
    )
    all_values = jnp.dot(ordering, all_values, preferred_element_type=jnp.float32).astype(
        jnp.bfloat16
    )

    experts = jnp.arange(ep_count, dtype=jnp.int32)
    named = route_ids.T[:, :, None] == experts[None, None, :]
    chosen = jnp.sum(named.astype(jnp.float32), axis=0)
    weights = jnp.sum(jnp.where(named, route_weights.T[:, :, None], 0.0), axis=0)
    token_index = jnp.arange(token_count, dtype=jnp.int32)
    before = (token_index[:, None] > token_index[None, :]).astype(jnp.float32)
    place = jnp.sum(before[:, :, None] * chosen[None, :, :], axis=1)
    place = jnp.where(chosen > 0, place, -1.0).astype(jnp.bfloat16)
    facts = jnp.concatenate([place, *three_terms(weights)], axis=1)
    facts_width = facts.shape[1]
    padded = -(-(facts_width + 3) // 128) * 128
    facts = jnp.pad(facts, ((0, 0), (0, padded - facts_width)))

    edges = split_edges(w_out.shape[1], PARTS)
    residuals, arrived = [], []
    squares = jnp.zeros((2, token_count, 1), jnp.float32)
    for part, (low, high) in enumerate(edges):
        array = (
            jnp.dot(all_values, w_out[:, low:high], preferred_element_type=jnp.float32)
            .astype(jnp.bfloat16)
            .reshape(ep_count, token_count, -1)
        )
        for step in range(bits - 1):
            total = halved(array, step, ep_count)
            array = total.astype(jnp.bfloat16)
        own = total[0] + hidden_in[:, low:high].astype(jnp.float32)
        total = jnp.stack([own, total[1]])
        sent = total.astype(jnp.bfloat16)
        last = part == len(edges) - 1
        if last:
            sent = jnp.concatenate([sent, jnp.stack([facts, jnp.zeros_like(facts)])], axis=2)
        got = lax.ppermute(sent, "ep", crossing(ep_count, bits - 1))
        if part == 0:
            gate_weights = fetched(w_gate[0], sent)
            up_weights = fetched(w_up[0], sent)
            got, gate_weights, up_weights = lax.optimization_barrier(
                (got, gate_weights, up_weights)
            )
        width = high - low
        if last:
            kept, array = normalised(facts_width, total, got, norm_gain[low:high], squares, facts)
        else:
            kept, array, more = normalised(facts_width, total, got, norm_gain[low:high])
            squares = squares + more
        residuals.append(kept)
        for step in range(bits - 2, -1, -1):
            array = doubled(array, step, ep_count)
        arrived.append(array.reshape(all_tokens, -1))
    facts = arrived[-1][:, width:].astype(jnp.float32)
    arrived[-1] = arrived[-1][:, :width]

    capacity = min(token_count, max(2, token_count * top_count * 9 // (8 * ep_count)))
    slots = ep_count * capacity
    mine = (experts == ep_rank).astype(jnp.float32)
    of_expert = [
        jnp.sum(facts[:, part * ep_count : (part + 1) * ep_count] * mine[None, :], axis=1)
        for part in range(4)
    ]
    token_place = of_expert[0].astype(jnp.int32)
    token_weight = of_expert[1] + of_expert[2] + of_expert[3]
    token_squares = jnp.sum(facts[:, 4 * ep_count : 4 * ep_count + 3], axis=1)
    if ctx_count == 2:
        token_squares = token_squares + lax.ppermute(token_squares, "ctx", swap)
    else:
        token_squares = lax.psum(token_squares, "ctx")
    token_scale = lax.rsqrt(token_squares / D + 1e-06)
    token_slot = jnp.where(token_place >= 0, chunk * capacity + token_place, -1)
    placing = jnp.arange(slots, dtype=jnp.int32)[:, None] == token_slot[None, :]
    slot_scale = jnp.sum(jnp.where(placing, token_scale[None, :], 0.0), axis=1)
    slot_weight = jnp.sum(jnp.where(placing, token_weight[None, :], 0.0), axis=1)
    placing = placing.astype(jnp.bfloat16)
    rows = [
        jnp.dot(placing, features, preferred_element_type=jnp.float32).astype(jnp.bfloat16)
        for features in arrived
    ]
    hidden = gate_weights.shape[1]
    ranges = split_edges(hidden, HIDDEN_PARTS)
    sums = []
    for start, stop in ranges:
        both = []
        for weights in (gate_weights, up_weights):
            total = 0.0
            for (low, high), part_rows in zip(edges, rows):
                total = total + jnp.dot(
                    part_rows, weights[low:high, start:stop], preferred_element_type=jnp.float32
                )
            both.append(total.astype(jnp.bfloat16))
        sums.append(jnp.concatenate(both, axis=1))
    if ctx_count == 2:
        others = [lax.ppermute(both, "ctx", swap) for both in sums]
        down_weights = fetched(w_down[0], sums[-1])
        others[0], down_weights = lax.optimization_barrier((others[0], down_weights))
        sums = [
            both.astype(jnp.float32) + other.astype(jnp.float32)
            for both, other in zip(sums, others)
        ]
    else:
        down_weights = w_down[0]
        sums = [lax.psum(both, "ctx").astype(jnp.float32) for both in sums]
    activated = []
    for both in sums:
        both = both * slot_scale[:, None]
        half = both.shape[1] // 2
        activated.append((jax.nn.silu(both[:, :half]) * both[:, half:]).astype(jnp.bfloat16))
    spread = placing.T
    outputs = []
    for (low, high), residual in zip(edges, residuals):
        produced = 0.0
        for (start, stop), part_rows in zip(ranges, activated):
            produced = produced + jnp.dot(
                part_rows, down_weights[start:stop, low:high], preferred_element_type=jnp.float32
            )
        produced = (produced * slot_weight[:, None]).astype(jnp.bfloat16)
        produced = lax.optimization_barrier(produced)
        array = (
            jnp.dot(spread, produced, preferred_element_type=jnp.float32)
            .astype(jnp.bfloat16)
            .reshape(ep_count, token_count, -1)
        )
        for step in range(bits):
            total = halved(array, step, ep_count)
            array = total.astype(jnp.bfloat16)
        outputs.append((residual + total[0]).astype(jnp.bfloat16))
    return jnp.concatenate(outputs, axis=1)


def solution(mesh):
    return jax.shard_map(
        shards,
        mesh=mesh,
        in_specs=(
            P("ctx", "ep"),
            P("ctx", None),
            P(),
            P("ep", None, None),
            P("ep", "ctx"),
            P("ep", "ctx"),
            P("ctx"),
            P("ep", None),
            P("ep", None),
            P("ep", "ctx", None),
            P("ep", "ctx", None),
            P("ep", None, "ctx"),
        ),
        out_specs=P("ep", "ctx"),
        check_vma=False,
    )
```

```python
import functools
import math

import jax
import jax.numpy as jnp
from jax import lax
from jax.experimental import pallas as pl
from jax.experimental.pallas import tpu as pltpu
from jax.sharding import PartitionSpec as P

D = 7168
KVL = 512


score_scale = (1.0 + 0.1 * math.log(40.0)) ** 2 / math.sqrt(192.0)
masked_score = -1e30
PARTS = 2
HIDDEN_PARTS = 2


def split_edges(width, parts):
    lanes = width // 128
    edges = [lanes * part // parts * 128 for part in range(parts)] + [width]
    return [(low, high) for low, high in zip(edges[:-1], edges[1:]) if high > low]


def split_columns(array, parts):
    return [array[..., low:high] for low, high in split_edges(array.shape[-1], parts)]


def step_bits(bits, lane):
    middle = list(range(1, bits - 1))
    if not lane:
        middle = middle[1:] + middle[:1]
    return [0] + middle + [bits - 1]


def crossing(count, step):
    bits = count.bit_length() - 1
    return [(index, index ^ (1 << step_bits(bits, index & 1)[step])) for index in range(count)]


def chunk_owners(count, rank, lane, number):
    bits = count.bit_length() - 1
    flip = number >> (bits - 1)
    distances = []
    for side in range(2):
        order = step_bits(bits, side)
        distance = jnp.zeros_like(number)
        for step in range(1, bits):
            distance = distance | ((number >> (bits - 1 - step)) & 1) << order[step]
        distances.append(distance)
    other_lane = (lane ^ flip) == 1
    return rank ^ flip ^ jnp.where(other_lane, distances[1], distances[0])


def halved(array, step, count):
    half = array.shape[0] // 2
    got = lax.ppermute(array[half:], "ep", crossing(count, step))
    return array[:half].astype(jnp.float32) + got.astype(jnp.float32)


def doubled(array, step, count):
    return jnp.concatenate([array, lax.ppermute(array, "ep", crossing(count, step))], axis=0)


def scores_kernel(
    pair_count,
    query_ref,
    keys_ref,
    up_ref,
    doc_ref,
    heads_ref,
    scores_ref,
    own_ref,
    up_out_ref,
    doc_out_ref,
):
    own_ref[...] = keys_ref[...]
    up_out_ref[...] = up_ref[...]
    doc_out_ref[...] = doc_ref[...]
    rows = query_ref.shape[0]
    pair_width = query_ref.shape[1] // pair_count
    width = heads_ref.shape[1]
    half = pair_count * rows
    for side in range(2):
        first = side * (pair_width - width)
        for pair in range(pair_count):
            at = side * half + pair * rows
            low = pair * pair_width + first
            heads_ref[at : at + rows, :] = query_ref[:, low : low + width]
        part = slice(side * half, (side + 1) * half)
        scores_ref[part, :] = jnp.dot(
            heads_ref[part, :], padded_keys(keys_ref, width, side), preferred_element_type=jnp.float32
        )


def padded_keys(keys_ref, width, side):
    zeros = jnp.zeros((width - keys_ref.shape[0], keys_ref.shape[1]), jnp.bfloat16)
    parts = [zeros, keys_ref[...]] if side else [keys_ref[...], zeros]
    return jnp.concatenate(parts, axis=0)


def attend_kernel(pair_count, doc_ref, heads_ref, scores_ref, up_ref, *refs):
    blocks, out_ref = refs[:-1], refs[-1]
    rows = out_ref.shape[0]
    half = pair_count * rows
    width = heads_ref.shape[1]
    value_width = up_ref.shape[2]
    rank = lax.axis_index("ctx")

    def docs_of(first, count):
        return doc_ref[:, pl.ds(pl.multiple_of(first, 128), count)]

    own_first = rank * rows
    query_doc = jnp.broadcast_to(docs_of(own_first, rows), (rows, rows)).T[:, 0:1]
    firsts = [jnp.int32(0)] if len(blocks) == 1 else [own_first, (1 - rank) * rows]
    scores, masks = [], []
    for first, block in zip(firsts, blocks):
        count = block.shape[1]
        key_pos = first + lax.broadcasted_iota(jnp.int32, (rows, count), 1)
        query_pos = own_first + lax.broadcasted_iota(jnp.int32, (rows, count), 0)
        allowed = (key_pos <= query_pos) & (docs_of(first, count) == query_doc)
        masks.append(jnp.where(allowed, 1.0, 0.0))
        if block is blocks[0]:
            scores.append(scores_ref[...])
        else:
            sides = [
                jnp.dot(
                    heads_ref[side * half : (side + 1) * half, :],
                    padded_keys(block, width, side),
                    preferred_element_type=jnp.float32,
                )
                for side in range(2)
            ]
            scores.append(jnp.concatenate(sides, axis=0))
    allowed = jnp.concatenate([jnp.concatenate(masks, axis=1)] * (2 * pair_count), axis=0) > 0
    scores = jnp.where(allowed, jnp.concatenate(scores, axis=1) * score_scale, masked_score)
    peak = jnp.max(scores, axis=1, keepdims=True)
    probs = jnp.where(allowed, jnp.exp(scores - peak), 0.0)
    total = jnp.sum(probs, axis=1, keepdims=True)
    context = lax.dot_general(
        probs.astype(jnp.bfloat16),
        jnp.concatenate([block[:KVL, :] for block in blocks], axis=1),
        (((1,), (1,)), ((), ())),
        preferred_element_type=jnp.float32,
    )
    context = (context / total).astype(jnp.bfloat16)
    for pair in range(pair_count):
        for side in range(2):
            at = side * half + pair * rows
            head = 2 * pair + side
            out_ref[:, head * value_width : (head + 1) * value_width] = jnp.dot(
                context[at : at + rows], up_ref[head], preferred_element_type=jnp.float32
            ).astype(jnp.bfloat16)


def whole_block(shape):
    return pl.BlockSpec(shape, lambda step: (0,) * len(shape))


def attend(queries, blocks, doc_ids, w_uv):
    rows = queries.shape[0]
    head_count, value_in, value_width = w_uv.shape
    query_width = queries.shape[1] // head_count
    key_count = doc_ids.shape[0]
    width = -(-query_width // 128) * 128
    pair_count = 2 if head_count % 4 == 0 and key_count <= 512 else 1
    heads = 2 * pair_count
    grid = (head_count // heads,)
    first_keys = blocks[0].shape[1]
    params = pltpu.CompilerParams(
        vmem_limit_bytes=(8 << 20) + 8 * heads * rows * (key_count + KVL) * 4
    )
    stacked = lambda columns: pl.BlockSpec((heads * rows, columns), lambda step: (step, 0))
    up_block = pl.BlockSpec((heads, value_in, value_width), lambda step: (step, 0, 0))
    arranged, scores, own, w_uv, docs = pl.pallas_call(
        functools.partial(scores_kernel, pair_count),
        out_shape=(
            jax.ShapeDtypeStruct((head_count * rows, width), jnp.bfloat16),
            jax.ShapeDtypeStruct((head_count * rows, first_keys), jnp.float32),
            jax.ShapeDtypeStruct(blocks[0].shape, jnp.bfloat16),
            jax.ShapeDtypeStruct(w_uv.shape, jnp.bfloat16),
            jax.ShapeDtypeStruct((1, key_count), jnp.int32),
        ),
        grid=grid,
        in_specs=[
            pl.BlockSpec((rows, heads * query_width), lambda step: (0, step)),
            whole_block(blocks[0].shape),
            up_block,
            whole_block((1, key_count)),
        ],
        out_specs=(
            stacked(width),
            stacked(first_keys),
            whole_block(blocks[0].shape),
            up_block,
            whole_block((1, key_count)),
        ),
        compiler_params=params,
        cost_estimate=pl.CostEstimate(
            flops=2 * rows * head_count * first_keys * width,
            bytes_accessed=2 * queries.size,
            transcendentals=0,
        ),
        name="first_scores",
    )(queries, blocks[0], w_uv, doc_ids[None])
    return pl.pallas_call(
        functools.partial(attend_kernel, pair_count),
        out_shape=jax.ShapeDtypeStruct((rows, head_count * value_width), jnp.bfloat16),
        grid=grid,
        in_specs=[
            whole_block((1, key_count)),
            stacked(width),
            stacked(first_keys),
            up_block,
            *(whole_block(block.shape) for block in blocks),
        ],
        out_specs=pl.BlockSpec((rows, heads * value_width), lambda step: (0, step)),
        compiler_params=params,
        cost_estimate=pl.CostEstimate(
            flops=2 * rows * head_count * key_count * (query_width + value_in),
            bytes_accessed=2 * (queries.size + w_uv.size),
            transcendentals=rows * head_count * key_count,
        ),
        name="attention",
    )(docs, arranged, scores, w_uv, own, *blocks[1:])


def fetch_kernel(pieces, first, from_ref, after_ref, to_ref, sems):
    rows = from_ref.shape[0] // pieces
    columns = pl.ds(first, to_ref.shape[1])
    copies = []
    for piece in range(pieces):
        part = pl.ds(piece * rows, rows)
        copies.append(
            pltpu.make_async_copy(
                from_ref.at[part, columns], to_ref.at[part], sems.at[piece]
            )
        )
    for copy in copies:
        copy.start()
    for copy in copies:
        copy.wait()


def fetched(weights, after, edges=None):
    pieces = 4
    low, high = edges or (0, weights.shape[1])
    return pl.pallas_call(
        functools.partial(fetch_kernel, pieces, low),
        out_shape=pltpu.VMEM((weights.shape[0], high - low), weights.dtype),
        in_specs=[
            pl.BlockSpec(memory_space=pltpu.HBM),
            pl.BlockSpec(memory_space=pl.ANY),
        ],
        out_specs=pl.BlockSpec(memory_space=pltpu.VMEM),
        scratch_shapes=[pltpu.SemaphoreType.DMA((pieces,))],
        compiler_params=pltpu.CompilerParams(vmem_limit_bytes=1 << 20),
        cost_estimate=pl.CostEstimate(
            flops=0, bytes_accessed=2 * weights.shape[0] * (high - low) * weights.dtype.itemsize, transcendentals=0
        ),
        name="fetch_weights",
    )(weights, after)


def norm_part(own_ref, got_ref, gain_ref, kept_ref, sent_ref):
    width = own_ref.shape[2]
    squares = []
    for chunk in range(2):
        residual = own_ref[chunk] + got_ref[1 - chunk, :, :width].astype(jnp.float32)
        if chunk == 0:
            kept_ref[...] = residual
        sent_ref[chunk, :, :width] = (residual * gain_ref[...]).astype(jnp.bfloat16)
        squares.append(jnp.sum(residual * residual, axis=1, keepdims=True))
    return squares


def first_norm_kernel(own_ref, got_ref, gain_ref, kept_ref, sent_ref, squares_ref):
    for chunk, squares in enumerate(norm_part(own_ref, got_ref, gain_ref, kept_ref, sent_ref)):
        squares_ref[chunk] = squares


def last_norm_kernel(
    facts_width, own_ref, got_ref, gain_ref, squares_ref, facts_ref, kept_ref, sent_ref
):
    width = own_ref.shape[2]
    for chunk, squares in enumerate(norm_part(own_ref, got_ref, gain_ref, kept_ref, sent_ref)):
        facts = facts_ref[...] if chunk == 0 else got_ref[0, :, width:]
        facts = facts.astype(jnp.float32)
        lane = lax.broadcasted_iota(jnp.int32, facts.shape, 1)
        for place, term in enumerate(three_terms(squares + squares_ref[chunk])):
            facts = jnp.where(lane == facts_width + place, term.astype(jnp.float32), facts)
        sent_ref[chunk, :, width:] = facts.astype(jnp.bfloat16)


def normalised(facts_width, own, got, gain, squares=None, facts=None):
    rows, width = own.shape[1:]
    vmem = pl.BlockSpec(memory_space=pltpu.VMEM)
    if squares is None:
        return pl.pallas_call(
            first_norm_kernel,
            out_shape=(
                jax.ShapeDtypeStruct((rows, width), jnp.float32),
                jax.ShapeDtypeStruct((2, rows, width), jnp.bfloat16),
                jax.ShapeDtypeStruct((2, rows, 1), jnp.float32),
            ),
            in_specs=[vmem] * 3,
            out_specs=(vmem,) * 3,
            compiler_params=pltpu.CompilerParams(vmem_limit_bytes=4 << 20),
            name="norm",
        )(own, got, gain[None])
    return pl.pallas_call(
        functools.partial(last_norm_kernel, facts_width),
        out_shape=(
            jax.ShapeDtypeStruct((rows, width), jnp.float32),
            jax.ShapeDtypeStruct((2, rows, width + facts.shape[1]), jnp.bfloat16),
        ),
        in_specs=[vmem] * 5,
        out_specs=(vmem,) * 2,
        compiler_params=pltpu.CompilerParams(vmem_limit_bytes=4 << 20),
        name="norm_last",
    )(own, got, gain[None], squares, facts)


def three_terms(values):
    first = values.astype(jnp.bfloat16)
    rest = values - first.astype(jnp.float32)
    second = rest.astype(jnp.bfloat16)
    third = (rest - second.astype(jnp.float32)).astype(jnp.bfloat16)
    return first, second, third


def shards(
    queries,
    latent,
    doc_ids,
    w_uv,
    w_out,
    hidden_in,
    norm_gain,
    route_ids,
    route_weights,
    w_gate,
    w_up,
    w_down,
):
    ctx_count = lax.axis_size("ctx")
    ep_count = lax.axis_size("ep")
    ctx_rank = lax.axis_index("ctx")
    ep_rank = lax.axis_index("ep")
    bits = ep_count.bit_length() - 1
    block_rows = queries.shape[0]
    token_count = hidden_in.shape[0]
    top_count = route_ids.shape[1]
    all_tokens = ep_count * token_count
    swap = [(0, 1), (1, 0)]

    key_columns, ctx_rank, ep_rank, lane = lax.optimization_barrier(
        (latent.T, ctx_rank, ep_rank, ep_rank & 1)
    )
    if ctx_count == 2:
        blocks = [key_columns, lax.ppermute(key_columns, "ctx", [(0, 1)])]
    else:
        blocks = [lax.all_gather(key_columns, "ctx", axis=1, tiled=True)]
    head_values = attend(queries, blocks, doc_ids, w_uv)
    route_ids, route_weights, norm_gain, head_values = lax.optimization_barrier(
        (route_ids, route_weights, norm_gain, head_values)
    )

    chunk = jnp.arange(all_tokens, dtype=jnp.int32) // token_count
    owner = chunk_owners(ep_count, ep_rank, lane, chunk)
    if ctx_count == 2:
        other = lax.ppermute(head_values, "ctx", swap)
        w_out = fetched(w_out, head_values)
        all_values = jnp.concatenate([head_values, other], axis=0)
        per_block = ep_count // 2
        owner = owner % per_block + per_block * (owner // per_block != ctx_rank)
    else:
        all_values = lax.all_gather(head_values, "ctx", axis=0, tiled=True)
    row = owner * token_count + jnp.arange(all_tokens, dtype=jnp.int32) % token_count
    ordering = (row[:, None] == jnp.arange(all_tokens, dtype=jnp.int32)[None, :]).astype(
        jnp.bfloat16
    )
    all_values = jnp.dot(ordering, all_values, preferred_element_type=jnp.float32).astype(
        jnp.bfloat16
    )

    experts = jnp.arange(ep_count, dtype=jnp.int32)
    named = route_ids.T[:, :, None] == experts[None, None, :]
    chosen = jnp.sum(named.astype(jnp.float32), axis=0)
    weights = jnp.sum(jnp.where(named, route_weights.T[:, :, None], 0.0), axis=0)
    token_index = jnp.arange(token_count, dtype=jnp.int32)
    before = (token_index[:, None] > token_index[None, :]).astype(jnp.float32)
    place = jnp.sum(before[:, :, None] * chosen[None, :, :], axis=1)
    place = jnp.where(chosen > 0, place, -1.0).astype(jnp.bfloat16)
    facts = jnp.concatenate([place, *three_terms(weights)], axis=1)
    facts_width = facts.shape[1]
    padded = -(-(facts_width + 3) // 128) * 128
    facts = jnp.pad(facts, ((0, 0), (0, padded - facts_width)))

    first_width = w_out.shape[1] // 128 * 15 // 28 * 128
    edges = [(0, first_width), (first_width, w_out.shape[1])]
    residuals, arrived = [], []
    squares = jnp.zeros((2, token_count, 1), jnp.float32)
    for part, (low, high) in enumerate(edges):
        array = (
            jnp.dot(all_values, w_out[:, low:high], preferred_element_type=jnp.float32)
            .astype(jnp.bfloat16)
            .reshape(ep_count, token_count, -1)
        )
        for step in range(bits - 1):
            total = halved(array, step, ep_count)
            array = total.astype(jnp.bfloat16)
        own = total[0] + hidden_in[:, low:high].astype(jnp.float32)
        total = jnp.stack([own, total[1]])
        sent = total.astype(jnp.bfloat16)
        last = part == len(edges) - 1
        if last:
            sent = jnp.concatenate([sent, jnp.stack([facts, jnp.zeros_like(facts)])], axis=2)
        got = lax.ppermute(sent, "ep", crossing(ep_count, bits - 1))
        if part == 0:
            gate_weights = fetched(w_gate[0], sent)
            up_weights = fetched(w_up[0], sent)
            got, gate_weights, up_weights = lax.optimization_barrier(
                (got, gate_weights, up_weights)
            )
        width = high - low
        if last:
            kept, array = normalised(facts_width, total, got, norm_gain[low:high], squares, facts)
        else:
            kept, array, more = normalised(facts_width, total, got, norm_gain[low:high])
            squares = squares + more
        residuals.append(kept)
        for step in range(bits - 2, -1, -1):
            array = doubled(array, step, ep_count)
        arrived.append(array.reshape(all_tokens, -1))
    facts = arrived[-1][:, width:].astype(jnp.float32)
    arrived[-1] = arrived[-1][:, :width]

    capacity = min(token_count, max(2, token_count * top_count * 9 // (8 * ep_count)))
    slots = ep_count * capacity
    mine = (experts == ep_rank).astype(jnp.float32)
    of_expert = [
        jnp.sum(facts[:, part * ep_count : (part + 1) * ep_count] * mine[None, :], axis=1)
        for part in range(4)
    ]
    token_place = of_expert[0].astype(jnp.int32)
    token_weight = of_expert[1] + of_expert[2] + of_expert[3]
    token_squares = jnp.sum(facts[:, 4 * ep_count : 4 * ep_count + 3], axis=1)
    if ctx_count == 2:
        token_squares = token_squares + lax.ppermute(token_squares, "ctx", swap)
    else:
        token_squares = lax.psum(token_squares, "ctx")
    token_scale = lax.rsqrt(token_squares / D + 1e-06)
    token_slot = jnp.where(token_place >= 0, chunk * capacity + token_place, -1)
    placing = jnp.arange(slots, dtype=jnp.int32)[:, None] == token_slot[None, :]
    slot_scale = jnp.sum(jnp.where(placing, token_scale[None, :], 0.0), axis=1)
    slot_weight = jnp.sum(jnp.where(placing, token_weight[None, :], 0.0), axis=1)
    placing = placing.astype(jnp.bfloat16)
    rows = [
        jnp.dot(placing, features, preferred_element_type=jnp.float32).astype(jnp.bfloat16)
        for features in arrived
    ]
    hidden = gate_weights.shape[1]
    ranges = split_edges(hidden, HIDDEN_PARTS)
    sums = []
    for start, stop in ranges:
        both = []
        for weights in (gate_weights, up_weights):
            total = 0.0
            for (low, high), part_rows in zip(edges, rows):
                total = total + jnp.dot(
                    part_rows, weights[low:high, start:stop], preferred_element_type=jnp.float32
                )
            both.append(total.astype(jnp.bfloat16))
        sums.append(jnp.concatenate(both, axis=1))
    if ctx_count == 2:
        others = [lax.ppermute(both, "ctx", swap) for both in sums]
        down_weights = fetched(w_down[0], sums[-1])
        others[0], down_weights = lax.optimization_barrier((others[0], down_weights))
        sums = [
            both.astype(jnp.float32) + other.astype(jnp.float32)
            for both, other in zip(sums, others)
        ]
    else:
        down_weights = w_down[0]
        sums = [lax.psum(both, "ctx").astype(jnp.float32) for both in sums]
    activated = []
    for both in sums:
        both = both * slot_scale[:, None]
        half = both.shape[1] // 2
        activated.append((jax.nn.silu(both[:, :half]) * both[:, half:]).astype(jnp.bfloat16))
    spread = placing.T
    outputs = []
    residuals = jnp.concatenate(residuals, axis=1)
    for low, high in split_edges(w_out.shape[1], PARTS):
        residual = residuals[:, low:high]
        produced = 0.0
        for (start, stop), part_rows in zip(ranges, activated):
            produced = produced + jnp.dot(
                part_rows, down_weights[start:stop, low:high], preferred_element_type=jnp.float32
            )
        produced = (produced * slot_weight[:, None]).astype(jnp.bfloat16)
        produced = lax.optimization_barrier(produced)
        array = (
            jnp.dot(spread, produced, preferred_element_type=jnp.float32)
            .astype(jnp.bfloat16)
            .reshape(ep_count, token_count, -1)
        )
        for step in range(bits):
            total = halved(array, step, ep_count)
            array = total.astype(jnp.bfloat16)
        outputs.append((residual + total[0]).astype(jnp.bfloat16))
    return jnp.concatenate(outputs, axis=1)


def solution(mesh):
    return jax.shard_map(
        shards,
        mesh=mesh,
        in_specs=(
            P("ctx", "ep"),
            P("ctx", None),
            P(),
            P("ep", None, None),
            P("ep", "ctx"),
            P("ep", "ctx"),
            P("ctx"),
            P("ep", None),
            P("ep", None),
            P("ep", "ctx", None),
            P("ep", "ctx", None),
            P("ep", None, "ctx"),
        ),
        out_specs=P("ep", "ctx"),
        check_vma=False,
    )
```

```python
import functools
import math

import jax
import jax.numpy as jnp
from jax import lax
from jax.experimental import pallas as pl
from jax.experimental.pallas import tpu as pltpu
from jax.sharding import PartitionSpec as P

D = 7168
KVL = 512


score_scale = (1.0 + 0.1 * math.log(40.0)) ** 2 / math.sqrt(192.0)
masked_score = -1e30
PARTS = 2
HIDDEN_PARTS = 2


def split_edges(width, parts):
    lanes = width // 128
    edges = [lanes * part // parts * 128 for part in range(parts)] + [width]
    return [(low, high) for low, high in zip(edges[:-1], edges[1:]) if high > low]


def split_columns(array, parts):
    return [array[..., low:high] for low, high in split_edges(array.shape[-1], parts)]


def step_bits(bits, lane):
    middle = list(range(1, bits - 1))
    if not lane:
        middle = middle[1:] + middle[:1]
    return [0] + middle + [bits - 1]


def crossing(count, step):
    bits = count.bit_length() - 1
    return [(index, index ^ (1 << step_bits(bits, index & 1)[step])) for index in range(count)]


def chunk_owners(count, rank, lane, number):
    bits = count.bit_length() - 1
    flip = number >> (bits - 1)
    distances = []
    for side in range(2):
        order = step_bits(bits, side)
        distance = jnp.zeros_like(number)
        for step in range(1, bits):
            distance = distance | ((number >> (bits - 1 - step)) & 1) << order[step]
        distances.append(distance)
    other_lane = (lane ^ flip) == 1
    return rank ^ flip ^ jnp.where(other_lane, distances[1], distances[0])


def halved(array, step, count):
    half = array.shape[0] // 2
    got = lax.ppermute(array[half:], "ep", crossing(count, step))
    return array[:half].astype(jnp.float32) + got.astype(jnp.float32)


def doubled(array, step, count):
    return jnp.concatenate([array, lax.ppermute(array, "ep", crossing(count, step))], axis=0)


def scores_kernel(
    pair_count,
    query_ref,
    keys_ref,
    up_ref,
    doc_ref,
    heads_ref,
    scores_ref,
    own_ref,
    up_out_ref,
    doc_out_ref,
):
    own_ref[...] = keys_ref[...]
    up_out_ref[...] = up_ref[...]
    doc_out_ref[...] = doc_ref[...]
    rows = query_ref.shape[0]
    pair_width = query_ref.shape[1] // pair_count
    width = heads_ref.shape[1]
    half = pair_count * rows
    for side in range(2):
        first = side * (pair_width - width)
        for pair in range(pair_count):
            at = side * half + pair * rows
            low = pair * pair_width + first
            heads_ref[at : at + rows, :] = query_ref[:, low : low + width]
        part = slice(side * half, (side + 1) * half)
        scores_ref[part, :] = jnp.dot(
            heads_ref[part, :], padded_keys(keys_ref, width, side), preferred_element_type=jnp.float32
        )


def padded_keys(keys_ref, width, side):
    zeros = jnp.zeros((width - keys_ref.shape[0], keys_ref.shape[1]), jnp.bfloat16)
    parts = [zeros, keys_ref[...]] if side else [keys_ref[...], zeros]
    return jnp.concatenate(parts, axis=0)


def attend_kernel(pair_count, doc_ref, heads_ref, scores_ref, up_ref, *refs):
    blocks, out_ref = refs[:-1], refs[-1]
    rows = out_ref.shape[0]
    half = pair_count * rows
    width = heads_ref.shape[1]
    value_width = up_ref.shape[2]
    rank = lax.axis_index("ctx")

    def docs_of(first, count):
        return doc_ref[:, pl.ds(pl.multiple_of(first, 128), count)]

    own_first = rank * rows
    query_doc = jnp.broadcast_to(docs_of(own_first, rows), (rows, rows)).T[:, 0:1]
    firsts = [jnp.int32(0)] if len(blocks) == 1 else [own_first, (1 - rank) * rows]
    scores, masks = [], []
    for first, block in zip(firsts, blocks):
        count = block.shape[1]
        key_pos = first + lax.broadcasted_iota(jnp.int32, (rows, count), 1)
        query_pos = own_first + lax.broadcasted_iota(jnp.int32, (rows, count), 0)
        allowed = (key_pos <= query_pos) & (docs_of(first, count) == query_doc)
        masks.append(jnp.where(allowed, 1.0, 0.0))
        if block is blocks[0]:
            scores.append(scores_ref[...])
        else:
            sides = [
                jnp.dot(
                    heads_ref[side * half : (side + 1) * half, :],
                    padded_keys(block, width, side),
                    preferred_element_type=jnp.float32,
                )
                for side in range(2)
            ]
            scores.append(jnp.concatenate(sides, axis=0))
    allowed = jnp.concatenate([jnp.concatenate(masks, axis=1)] * (2 * pair_count), axis=0) > 0
    scores = jnp.where(allowed, jnp.concatenate(scores, axis=1) * score_scale, masked_score)
    peak = jnp.max(scores, axis=1, keepdims=True)
    probs = jnp.where(allowed, jnp.exp(scores - peak), 0.0)
    total = jnp.sum(probs, axis=1, keepdims=True)
    context = lax.dot_general(
        probs.astype(jnp.bfloat16),
        jnp.concatenate([block[:KVL, :] for block in blocks], axis=1),
        (((1,), (1,)), ((), ())),
        preferred_element_type=jnp.float32,
    )
    context = (context / total).astype(jnp.bfloat16)
    for pair in range(pair_count):
        for side in range(2):
            at = side * half + pair * rows
            head = 2 * pair + side
            out_ref[:, head * value_width : (head + 1) * value_width] = jnp.dot(
                context[at : at + rows], up_ref[head], preferred_element_type=jnp.float32
            ).astype(jnp.bfloat16)


def whole_block(shape):
    return pl.BlockSpec(shape, lambda step: (0,) * len(shape))


def attend(queries, blocks, doc_ids, w_uv):
    rows = queries.shape[0]
    head_count, value_in, value_width = w_uv.shape
    query_width = queries.shape[1] // head_count
    key_count = doc_ids.shape[0]
    width = -(-query_width // 128) * 128
    pair_count = 2 if head_count % 4 == 0 and key_count <= 512 else 1
    heads = 2 * pair_count
    grid = (head_count // heads,)
    first_keys = blocks[0].shape[1]
    params = pltpu.CompilerParams(
        vmem_limit_bytes=(8 << 20) + 8 * heads * rows * (key_count + KVL) * 4
    )
    stacked = lambda columns: pl.BlockSpec((heads * rows, columns), lambda step: (step, 0))
    up_block = pl.BlockSpec((heads, value_in, value_width), lambda step: (step, 0, 0))
    arranged, scores, own, w_uv, docs = pl.pallas_call(
        functools.partial(scores_kernel, pair_count),
        out_shape=(
            jax.ShapeDtypeStruct((head_count * rows, width), jnp.bfloat16),
            jax.ShapeDtypeStruct((head_count * rows, first_keys), jnp.float32),
            jax.ShapeDtypeStruct(blocks[0].shape, jnp.bfloat16),
            jax.ShapeDtypeStruct(w_uv.shape, jnp.bfloat16),
            jax.ShapeDtypeStruct((1, key_count), jnp.int32),
        ),
        grid=grid,
        in_specs=[
            pl.BlockSpec((rows, heads * query_width), lambda step: (0, step)),
            whole_block(blocks[0].shape),
            up_block,
            whole_block((1, key_count)),
        ],
        out_specs=(
            stacked(width),
            stacked(first_keys),
            whole_block(blocks[0].shape),
            up_block,
            whole_block((1, key_count)),
        ),
        compiler_params=params,
        cost_estimate=pl.CostEstimate(
            flops=2 * rows * head_count * first_keys * width,
            bytes_accessed=2 * queries.size,
            transcendentals=0,
        ),
        name="first_scores",
    )(queries, blocks[0], w_uv, doc_ids[None])
    return pl.pallas_call(
        functools.partial(attend_kernel, pair_count),
        out_shape=jax.ShapeDtypeStruct((rows, head_count * value_width), jnp.bfloat16),
        grid=grid,
        in_specs=[
            whole_block((1, key_count)),
            stacked(width),
            stacked(first_keys),
            up_block,
            *(whole_block(block.shape) for block in blocks),
        ],
        out_specs=pl.BlockSpec((rows, heads * value_width), lambda step: (0, step)),
        compiler_params=params,
        cost_estimate=pl.CostEstimate(
            flops=2 * rows * head_count * key_count * (query_width + value_in),
            bytes_accessed=2 * (queries.size + w_uv.size),
            transcendentals=rows * head_count * key_count,
        ),
        name="attention",
    )(docs, arranged, scores, w_uv, own, *blocks[1:])


def fetch_kernel(pieces, first, from_ref, after_ref, to_ref, sems):
    rows = from_ref.shape[0] // pieces
    columns = pl.ds(first, to_ref.shape[1])
    copies = []
    for piece in range(pieces):
        part = pl.ds(piece * rows, rows)
        copies.append(
            pltpu.make_async_copy(
                from_ref.at[part, columns], to_ref.at[part], sems.at[piece]
            )
        )
    for copy in copies:
        copy.start()
    for copy in copies:
        copy.wait()


def fetched(weights, after, edges=None):
    pieces = 4
    low, high = edges or (0, weights.shape[1])
    return pl.pallas_call(
        functools.partial(fetch_kernel, pieces, low),
        out_shape=pltpu.VMEM((weights.shape[0], high - low), weights.dtype),
        in_specs=[
            pl.BlockSpec(memory_space=pltpu.HBM),
            pl.BlockSpec(memory_space=pl.ANY),
        ],
        out_specs=pl.BlockSpec(memory_space=pltpu.VMEM),
        scratch_shapes=[pltpu.SemaphoreType.DMA((pieces,))],
        compiler_params=pltpu.CompilerParams(vmem_limit_bytes=1 << 20),
        cost_estimate=pl.CostEstimate(
            flops=0, bytes_accessed=2 * weights.shape[0] * (high - low) * weights.dtype.itemsize, transcendentals=0
        ),
        name="fetch_weights",
    )(weights, after)


def norm_part(own_ref, got_ref, gain_ref, kept_ref, sent_ref):
    width = own_ref.shape[2]
    squares = []
    for chunk in range(2):
        residual = own_ref[chunk] + got_ref[1 - chunk, :, :width].astype(jnp.float32)
        if chunk == 0:
            kept_ref[...] = residual
        sent_ref[chunk, :, :width] = (residual * gain_ref[...]).astype(jnp.bfloat16)
        squares.append(jnp.sum(residual * residual, axis=1, keepdims=True))
    return squares


def first_norm_kernel(own_ref, got_ref, gain_ref, kept_ref, sent_ref, squares_ref):
    for chunk, squares in enumerate(norm_part(own_ref, got_ref, gain_ref, kept_ref, sent_ref)):
        squares_ref[chunk] = squares


def last_norm_kernel(
    facts_width, own_ref, got_ref, gain_ref, squares_ref, facts_ref, kept_ref, sent_ref
):
    width = own_ref.shape[2]
    for chunk, squares in enumerate(norm_part(own_ref, got_ref, gain_ref, kept_ref, sent_ref)):
        facts = facts_ref[...] if chunk == 0 else got_ref[0, :, width:]
        facts = facts.astype(jnp.float32)
        lane = lax.broadcasted_iota(jnp.int32, facts.shape, 1)
        for place, term in enumerate(three_terms(squares + squares_ref[chunk])):
            facts = jnp.where(lane == facts_width + place, term.astype(jnp.float32), facts)
        sent_ref[chunk, :, width:] = facts.astype(jnp.bfloat16)


def normalised(facts_width, own, got, gain, squares=None, facts=None):
    rows, width = own.shape[1:]
    vmem = pl.BlockSpec(memory_space=pltpu.VMEM)
    if squares is None:
        return pl.pallas_call(
            first_norm_kernel,
            out_shape=(
                jax.ShapeDtypeStruct((rows, width), jnp.float32),
                jax.ShapeDtypeStruct((2, rows, width), jnp.bfloat16),
                jax.ShapeDtypeStruct((2, rows, 1), jnp.float32),
            ),
            in_specs=[vmem] * 3,
            out_specs=(vmem,) * 3,
            compiler_params=pltpu.CompilerParams(vmem_limit_bytes=4 << 20),
            name="norm",
        )(own, got, gain[None])
    return pl.pallas_call(
        functools.partial(last_norm_kernel, facts_width),
        out_shape=(
            jax.ShapeDtypeStruct((rows, width), jnp.float32),
            jax.ShapeDtypeStruct((2, rows, width + facts.shape[1]), jnp.bfloat16),
        ),
        in_specs=[vmem] * 5,
        out_specs=(vmem,) * 2,
        compiler_params=pltpu.CompilerParams(vmem_limit_bytes=4 << 20),
        name="norm_last",
    )(own, got, gain[None], squares, facts)


def project_kernel(edge, values_ref, weights_ref, out_ref):
    low, high = edge
    out_ref[...] = jnp.dot(
        values_ref[...], weights_ref[:, low:high], preferred_element_type=jnp.float32
    ).astype(jnp.bfloat16)


def project(values, weights, edge):
    vmem = pl.BlockSpec(memory_space=pltpu.VMEM)
    return pl.pallas_call(
        functools.partial(project_kernel, edge),
        out_shape=jax.ShapeDtypeStruct((values.shape[0], edge[1] - edge[0]), jnp.bfloat16),
        in_specs=[vmem] * 2,
        out_specs=vmem,
        compiler_params=pltpu.CompilerParams(vmem_limit_bytes=8 << 20),
        cost_estimate=pl.CostEstimate(flops=0, bytes_accessed=0, transcendentals=0),
        name="project",
    )(values, weights)


def terms_kernel(edges, hidden_range, *refs):
    row_refs, (gate_ref, up_ref, *more, out_ref) = refs[: len(edges)], refs[len(edges) :]
    start, stop = hidden_range
    for place, weights_ref in enumerate((gate_ref, up_ref)):
        total = 0.0
        for (low, high), row_ref in zip(edges, row_refs):
            total = total + jnp.dot(
                row_ref[...], weights_ref[low:high, start:stop], preferred_element_type=jnp.float32
            )
        width = stop - start
        out_ref[:, place * width : (place + 1) * width] = total.astype(jnp.bfloat16)
    if more:
        placing_ref, facts_ref = more
        out_ref[:, 2 * width :] = jnp.dot(
            placing_ref[...], facts_ref[...], preferred_element_type=jnp.float32
        ).astype(jnp.bfloat16)


def hidden_terms(rows, edges, hidden_range, gate_weights, up_weights, *facts):
    vmem = pl.BlockSpec(memory_space=pltpu.VMEM)
    width = 2 * (hidden_range[1] - hidden_range[0]) + (facts[1].shape[1] if facts else 0)
    return pl.pallas_call(
        functools.partial(terms_kernel, edges, hidden_range),
        out_shape=jax.ShapeDtypeStruct((rows[0].shape[0], width), jnp.bfloat16),
        in_specs=[vmem] * (len(rows) + 2 + len(facts)),
        out_specs=vmem,
        compiler_params=pltpu.CompilerParams(vmem_limit_bytes=8 << 20),
        cost_estimate=pl.CostEstimate(flops=0, bytes_accessed=0, transcendentals=0),
        name="hidden_terms",
    )(*rows, gate_weights, up_weights, *facts)


def three_terms(values):
    first = values.astype(jnp.bfloat16)
    rest = values - first.astype(jnp.float32)
    second = rest.astype(jnp.bfloat16)
    third = (rest - second.astype(jnp.float32)).astype(jnp.bfloat16)
    return first, second, third


def shards(
    queries,
    latent,
    doc_ids,
    w_uv,
    w_out,
    hidden_in,
    norm_gain,
    route_ids,
    route_weights,
    w_gate,
    w_up,
    w_down,
):
    ctx_count = lax.axis_size("ctx")
    ep_count = lax.axis_size("ep")
    ctx_rank = lax.axis_index("ctx")
    ep_rank = lax.axis_index("ep")
    bits = ep_count.bit_length() - 1
    block_rows = queries.shape[0]
    token_count = hidden_in.shape[0]
    top_count = route_ids.shape[1]
    all_tokens = ep_count * token_count
    swap = [(0, 1), (1, 0)]

    key_columns, ctx_rank, ep_rank, lane = lax.optimization_barrier(
        (latent.T, ctx_rank, ep_rank, ep_rank & 1)
    )
    if ctx_count == 2:
        blocks = [key_columns, lax.ppermute(key_columns, "ctx", [(0, 1)])]
    else:
        blocks = [lax.all_gather(key_columns, "ctx", axis=1, tiled=True)]
    head_values = attend(queries, blocks, doc_ids, w_uv)
    route_ids, route_weights, norm_gain, head_values = lax.optimization_barrier(
        (route_ids, route_weights, norm_gain, head_values)
    )

    chunk = jnp.arange(all_tokens, dtype=jnp.int32) // token_count
    owner = chunk_owners(ep_count, ep_rank, lane, chunk)
    if ctx_count == 2:
        other = lax.ppermute(head_values, "ctx", swap)
        w_out = fetched(w_out, head_values)
        all_values = jnp.concatenate([head_values, other], axis=0)
        per_block = ep_count // 2
        owner = owner % per_block + per_block * (owner // per_block != ctx_rank)
    else:
        all_values = lax.all_gather(head_values, "ctx", axis=0, tiled=True)
    row = owner * token_count + jnp.arange(all_tokens, dtype=jnp.int32) % token_count
    ordering = (row[:, None] == jnp.arange(all_tokens, dtype=jnp.int32)[None, :]).astype(
        jnp.bfloat16
    )
    all_values = jnp.dot(ordering, all_values, preferred_element_type=jnp.float32).astype(
        jnp.bfloat16
    )

    experts = jnp.arange(ep_count, dtype=jnp.int32)
    named = route_ids.T[:, :, None] == experts[None, None, :]
    chosen = jnp.sum(named.astype(jnp.float32), axis=0)
    weights = jnp.sum(jnp.where(named, route_weights.T[:, :, None], 0.0), axis=0)
    token_index = jnp.arange(token_count, dtype=jnp.int32)
    before = (token_index[:, None] > token_index[None, :]).astype(jnp.float32)
    place = jnp.sum(before[:, :, None] * chosen[None, :, :], axis=1)
    place = jnp.where(chosen > 0, place, -1.0).astype(jnp.bfloat16)
    facts = jnp.concatenate([place, *three_terms(weights)], axis=1)
    facts_width = facts.shape[1]
    padded = -(-(facts_width + 3) // 128) * 128
    facts = jnp.pad(facts, ((0, 0), (0, padded - facts_width)))

    first_width = w_out.shape[1] // 128 * 15 // 28 * 128
    edges = [(0, first_width), (first_width, w_out.shape[1])]
    residuals, arrived = [], []
    squares = jnp.zeros((2, token_count, 1), jnp.float32)
    for part, (low, high) in enumerate(edges):
        array = project(all_values, w_out, (low, high))
        if part == 0:
            all_values, array = lax.optimization_barrier((all_values, array))
        array = array.reshape(ep_count, token_count, -1)
        for step in range(bits - 1):
            total = halved(array, step, ep_count)
            array = total.astype(jnp.bfloat16)
        own = total[0] + hidden_in[:, low:high].astype(jnp.float32)
        total = jnp.stack([own, total[1]])
        sent = total.astype(jnp.bfloat16)
        last = part == len(edges) - 1
        if last:
            sent = jnp.concatenate([sent, jnp.stack([facts, jnp.zeros_like(facts)])], axis=2)
        got = lax.ppermute(sent, "ep", crossing(ep_count, bits - 1))
        if part == 0:
            gate_weights = fetched(w_gate[0], sent)
            up_weights = fetched(w_up[0], sent)
            got, gate_weights, up_weights = lax.optimization_barrier(
                (got, gate_weights, up_weights)
            )
        width = high - low
        if last:
            kept, array = normalised(facts_width, total, got, norm_gain[low:high], squares, facts)
        else:
            kept, array, more = normalised(facts_width, total, got, norm_gain[low:high])
            squares = squares + more
        residuals.append(kept)
        for step in range(bits - 2, -1, -1):
            array = doubled(array, step, ep_count)
        arrived.append(array.reshape(all_tokens, -1))
    all_facts = arrived[-1][:, width:]
    facts = all_facts.astype(jnp.float32)
    arrived[-1] = arrived[-1][:, :width]

    capacity = min(token_count, max(2, token_count * top_count * 9 // (8 * ep_count)))
    slots = ep_count * capacity
    mine = (experts == ep_rank).astype(jnp.float32)
    of_expert = [
        jnp.sum(facts[:, part * ep_count : (part + 1) * ep_count] * mine[None, :], axis=1)
        for part in range(4)
    ]
    token_place = of_expert[0].astype(jnp.int32)
    token_weight = of_expert[1] + of_expert[2] + of_expert[3]
    token_squares = jnp.sum(facts[:, 4 * ep_count : 4 * ep_count + 3], axis=1)
    token_slot = jnp.where(token_place >= 0, chunk * capacity + token_place, -1)
    placing = jnp.arange(slots, dtype=jnp.int32)[:, None] == token_slot[None, :]
    slot_weight = jnp.sum(jnp.where(placing, token_weight[None, :], 0.0), axis=1)
    placed, placing = placing, placing.astype(jnp.bfloat16)
    rows = [
        jnp.dot(placing, features, preferred_element_type=jnp.float32).astype(jnp.bfloat16)
        for features in arrived
    ]
    hidden = gate_weights.shape[1]
    ranges = split_edges(hidden, HIDDEN_PARTS)
    sums = []
    for hidden_range in ranges:
        beside = (placing, all_facts) if hidden_range is ranges[0] and ctx_count == 2 else ()
        sums.append(hidden_terms(rows, edges, hidden_range, gate_weights, up_weights, *beside))
        if hidden_range is ranges[0]:
            rows[0], sums[0] = lax.optimization_barrier((rows[0], sums[0]))
    if ctx_count == 2:
        others = [lax.ppermute(both, "ctx", swap) for both in sums]
        down_weights = fetched(w_down[0], sums[-1])
        others[0], down_weights = lax.optimization_barrier((others[0], down_weights))
        squares_at = 2 * ranges[0][1] + facts_width
    else:
        down_weights = w_down[0]
        others = [
            lax.psum(both, "ctx").astype(jnp.float32) - both.astype(jnp.float32) for both in sums
        ]
        squares = jnp.where(placed, lax.psum(token_squares, "ctx")[None, :], 0.0)
        slot_squares = jnp.sum(squares, axis=1, keepdims=True)
    out_edges = split_edges(w_out.shape[1], PARTS)
    activated = []
    for place in range(len(ranges)):
        if place == 1:
            others[1], first_products = lax.optimization_barrier((others[1], first_products))
        both = sums[place].astype(jnp.float32) + others[place].astype(jnp.float32)
        if place == 0:
            if ctx_count == 2:
                terms = both[:, squares_at : squares_at + 3]
                slot_squares = jnp.sum(terms, axis=1, keepdims=True)
            slot_scale = lax.rsqrt(slot_squares / D + 1e-06)
        half = ranges[place][1] - ranges[place][0]
        both = both[:, : 2 * half] * slot_scale
        weighted = both[:, half:] * slot_weight[:, None]
        activated.append((jax.nn.silu(both[:, :half]) * weighted).astype(jnp.bfloat16))
        if place == 0:
            start, stop = ranges[0]
            first_products = [
                jnp.dot(
                    activated[0],
                    down_weights[start:stop, low:high],
                    preferred_element_type=jnp.float32,
                )
                for low, high in out_edges
            ]
    spread = placing.T
    outputs = []
    residuals = jnp.concatenate(residuals, axis=1)
    for (low, high), produced in zip(out_edges, first_products):
        residual = residuals[:, low:high]
        for (start, stop), part_rows in zip(ranges[1:], activated[1:]):
            produced = produced + jnp.dot(
                part_rows, down_weights[start:stop, low:high], preferred_element_type=jnp.float32
            )
        produced = produced.astype(jnp.bfloat16)
        produced = lax.optimization_barrier(produced)
        array = (
            jnp.dot(spread, produced, preferred_element_type=jnp.float32)
            .astype(jnp.bfloat16)
            .reshape(ep_count, token_count, -1)
        )
        for step in range(bits):
            total = halved(array, step, ep_count)
            array = total.astype(jnp.bfloat16)
        outputs.append((residual + total[0]).astype(jnp.bfloat16))
    return jnp.concatenate(outputs, axis=1)


def solution(mesh):
    return jax.shard_map(
        shards,
        mesh=mesh,
        in_specs=(
            P("ctx", "ep"),
            P("ctx", None),
            P(),
            P("ep", None, None),
            P("ep", "ctx"),
            P("ep", "ctx"),
            P("ctx"),
            P("ep", None),
            P("ep", None),
            P("ep", "ctx", None),
            P("ep", "ctx", None),
            P("ep", None, "ctx"),
        ),
        out_specs=P("ep", "ctx"),
        check_vma=False,
    )
```

```python
import functools
import math

import jax
import jax.numpy as jnp
from jax import lax
from jax.experimental import pallas as pl
from jax.experimental.pallas import tpu as pltpu
from jax.sharding import PartitionSpec as P

D = 7168
KVL = 512


score_scale = (1.0 + 0.1 * math.log(40.0)) ** 2 / math.sqrt(192.0)
masked_score = -1e30
PARTS = 2
HIDDEN_PARTS = 2


def split_edges(width, parts):
    lanes = width // 128
    edges = [lanes * part // parts * 128 for part in range(parts)] + [width]
    return [(low, high) for low, high in zip(edges[:-1], edges[1:]) if high > low]


def split_columns(array, parts):
    return [array[..., low:high] for low, high in split_edges(array.shape[-1], parts)]


def step_bits(bits, lane):
    middle = list(range(1, bits - 1))
    if not lane:
        middle = middle[1:] + middle[:1]
    return [0] + middle + [bits - 1]


def crossing(count, step):
    bits = count.bit_length() - 1
    return [(index, index ^ (1 << step_bits(bits, index & 1)[step])) for index in range(count)]


def chunk_owners(count, rank, lane, number):
    bits = count.bit_length() - 1
    flip = number >> (bits - 1)
    distances = []
    for side in range(2):
        order = step_bits(bits, side)
        distance = jnp.zeros_like(number)
        for step in range(1, bits):
            distance = distance | ((number >> (bits - 1 - step)) & 1) << order[step]
        distances.append(distance)
    other_lane = (lane ^ flip) == 1
    return rank ^ flip ^ jnp.where(other_lane, distances[1], distances[0])


def halved(array, step, count):
    half = array.shape[0] // 2
    got = lax.ppermute(array[half:], "ep", crossing(count, step))
    return array[:half].astype(jnp.float32) + got.astype(jnp.float32)


def doubled(array, step, count):
    return jnp.concatenate([array, lax.ppermute(array, "ep", crossing(count, step))], axis=0)


def scores_kernel(
    pair_count,
    query_ref,
    keys_ref,
    up_ref,
    doc_ref,
    heads_ref,
    scores_ref,
    own_ref,
    up_out_ref,
    doc_out_ref,
):
    own_ref[...] = keys_ref[...]
    up_out_ref[...] = up_ref[...]
    doc_out_ref[...] = doc_ref[...]
    rows = query_ref.shape[0]
    pair_width = query_ref.shape[1] // pair_count
    width = heads_ref.shape[1]
    half = pair_count * rows
    for side in range(2):
        first = side * (pair_width - width)
        for pair in range(pair_count):
            at = side * half + pair * rows
            low = pair * pair_width + first
            heads_ref[at : at + rows, :] = query_ref[:, low : low + width]
        part = slice(side * half, (side + 1) * half)
        scores_ref[part, :] = jnp.dot(
            heads_ref[part, :], padded_keys(keys_ref, width, side), preferred_element_type=jnp.float32
        )


def padded_keys(keys_ref, width, side):
    zeros = jnp.zeros((width - keys_ref.shape[0], keys_ref.shape[1]), jnp.bfloat16)
    parts = [zeros, keys_ref[...]] if side else [keys_ref[...], zeros]
    return jnp.concatenate(parts, axis=0)


def attend_kernel(pair_count, doc_ref, heads_ref, scores_ref, up_ref, *refs):
    blocks, out_ref = refs[:-1], refs[-1]
    rows = out_ref.shape[0]
    half = pair_count * rows
    width = heads_ref.shape[1]
    value_width = up_ref.shape[2]
    rank = lax.axis_index("ctx")

    def docs_of(first, count):
        return doc_ref[:, pl.ds(pl.multiple_of(first, 128), count)]

    own_first = rank * rows
    query_doc = jnp.broadcast_to(docs_of(own_first, rows), (rows, rows)).T[:, 0:1]
    firsts = [jnp.int32(0)] if len(blocks) == 1 else [own_first, (1 - rank) * rows]
    scores, masks = [], []
    for first, block in zip(firsts, blocks):
        count = block.shape[1]
        key_pos = first + lax.broadcasted_iota(jnp.int32, (rows, count), 1)
        query_pos = own_first + lax.broadcasted_iota(jnp.int32, (rows, count), 0)
        allowed = (key_pos <= query_pos) & (docs_of(first, count) == query_doc)
        masks.append(jnp.where(allowed, 1.0, 0.0))
        if block is blocks[0]:
            scores.append(scores_ref[...])
        else:
            sides = [
                jnp.dot(
                    heads_ref[side * half : (side + 1) * half, :],
                    padded_keys(block, width, side),
                    preferred_element_type=jnp.float32,
                )
                for side in range(2)
            ]
            scores.append(jnp.concatenate(sides, axis=0))
    allowed = jnp.concatenate([jnp.concatenate(masks, axis=1)] * (2 * pair_count), axis=0) > 0
    scores = jnp.where(allowed, jnp.concatenate(scores, axis=1) * score_scale, masked_score)
    peak = jnp.max(scores, axis=1, keepdims=True)
    probs = jnp.where(allowed, jnp.exp(scores - peak), 0.0)
    total = jnp.sum(probs, axis=1, keepdims=True)
    context = lax.dot_general(
        probs.astype(jnp.bfloat16),
        jnp.concatenate([block[:KVL, :] for block in blocks], axis=1),
        (((1,), (1,)), ((), ())),
        preferred_element_type=jnp.float32,
    )
    context = (context / total).astype(jnp.bfloat16)
    for pair in range(pair_count):
        for side in range(2):
            at = side * half + pair * rows
            head = 2 * pair + side
            out_ref[:, head * value_width : (head + 1) * value_width] = jnp.dot(
                context[at : at + rows], up_ref[head], preferred_element_type=jnp.float32
            ).astype(jnp.bfloat16)


def whole_block(shape):
    return pl.BlockSpec(shape, lambda step: (0,) * len(shape))


def in_vmem(grid, spec):
    return spec if grid else pl.BlockSpec(memory_space=pltpu.VMEM)


def attend(queries, blocks, doc_ids, w_uv):
    rows = queries.shape[0]
    head_count, value_in, value_width = w_uv.shape
    query_width = queries.shape[1] // head_count
    key_count = doc_ids.shape[0]
    width = -(-query_width // 128) * 128
    pair_count = head_count // 2 if key_count <= 512 else 1
    heads = 2 * pair_count
    grid = (head_count // heads,) if head_count > heads else ()
    first_keys = blocks[0].shape[1]
    params = pltpu.CompilerParams(
        vmem_limit_bytes=(8 << 20) + 8 * heads * rows * (key_count + KVL) * 4
    )
    stacked = lambda columns: pl.BlockSpec((heads * rows, columns), lambda step: (step, 0))
    up_block = pl.BlockSpec((heads, value_in, value_width), lambda step: (step, 0, 0))
    arranged, scores, own, w_uv, docs = pl.pallas_call(
        functools.partial(scores_kernel, pair_count),
        out_shape=(
            jax.ShapeDtypeStruct((head_count * rows, width), jnp.bfloat16),
            jax.ShapeDtypeStruct((head_count * rows, first_keys), jnp.float32),
            jax.ShapeDtypeStruct(blocks[0].shape, jnp.bfloat16),
            jax.ShapeDtypeStruct(w_uv.shape, jnp.bfloat16),
            jax.ShapeDtypeStruct((1, key_count), jnp.int32),
        ),
        grid=grid,
        in_specs=[
            in_vmem(grid, spec)
            for spec in (
                pl.BlockSpec((rows, heads * query_width), lambda step: (0, step)),
                whole_block(blocks[0].shape),
                up_block,
                whole_block((1, key_count)),
            )
        ],
        out_specs=tuple(
            in_vmem(grid, spec)
            for spec in (
                stacked(width),
                stacked(first_keys),
                whole_block(blocks[0].shape),
                up_block,
                whole_block((1, key_count)),
            )
        ),
        compiler_params=params,
        cost_estimate=pl.CostEstimate(
            flops=2 * rows * head_count * first_keys * width,
            bytes_accessed=2 * queries.size,
            transcendentals=0,
        ),
        name="first_scores",
    )(queries, blocks[0], w_uv, doc_ids[None])
    return pl.pallas_call(
        functools.partial(attend_kernel, pair_count),
        out_shape=jax.ShapeDtypeStruct((rows, head_count * value_width), jnp.bfloat16),
        grid=grid,
        in_specs=[
            in_vmem(grid, spec)
            for spec in (
                whole_block((1, key_count)),
                stacked(width),
                stacked(first_keys),
                up_block,
                *(whole_block(block.shape) for block in blocks),
            )
        ],
        out_specs=in_vmem(
            grid, pl.BlockSpec((rows, heads * value_width), lambda step: (0, step))
        ),
        compiler_params=params,
        cost_estimate=pl.CostEstimate(
            flops=2 * rows * head_count * key_count * (query_width + value_in),
            bytes_accessed=2 * (queries.size + w_uv.size),
            transcendentals=rows * head_count * key_count,
        ),
        name="attention",
    )(docs, arranged, scores, w_uv, own, *blocks[1:])


def fetch_kernel(pieces, first, from_ref, after_ref, to_ref, sems):
    rows = from_ref.shape[0] // pieces
    columns = pl.ds(first, to_ref.shape[1])
    copies = []
    for piece in range(pieces):
        part = pl.ds(piece * rows, rows)
        copies.append(
            pltpu.make_async_copy(
                from_ref.at[part, columns], to_ref.at[part], sems.at[piece]
            )
        )
    for copy in copies:
        copy.start()
    for copy in copies:
        copy.wait()


def fetched(weights, after, edges=None):
    pieces = 4
    low, high = edges or (0, weights.shape[1])
    return pl.pallas_call(
        functools.partial(fetch_kernel, pieces, low),
        out_shape=pltpu.VMEM((weights.shape[0], high - low), weights.dtype),
        in_specs=[
            pl.BlockSpec(memory_space=pltpu.HBM),
            pl.BlockSpec(memory_space=pl.ANY),
        ],
        out_specs=pl.BlockSpec(memory_space=pltpu.VMEM),
        scratch_shapes=[pltpu.SemaphoreType.DMA((pieces,))],
        compiler_params=pltpu.CompilerParams(vmem_limit_bytes=1 << 20),
        cost_estimate=pl.CostEstimate(flops=0, bytes_accessed=0, transcendentals=0),
        name="fetch_weights",
    )(weights, after)


def norm_part(own_ref, got_ref, gain_ref, kept_ref, sent_ref):
    width = own_ref.shape[2]
    squares = []
    for chunk in range(2):
        residual = own_ref[chunk] + got_ref[1 - chunk, :, :width].astype(jnp.float32)
        if chunk == 0:
            kept_ref[...] = residual
        sent_ref[chunk, :, :width] = (residual * gain_ref[...]).astype(jnp.bfloat16)
        squares.append(jnp.sum(residual * residual, axis=1, keepdims=True))
    return squares


def first_norm_kernel(own_ref, got_ref, gain_ref, kept_ref, sent_ref, squares_ref):
    for chunk, squares in enumerate(norm_part(own_ref, got_ref, gain_ref, kept_ref, sent_ref)):
        squares_ref[chunk] = squares


def last_norm_kernel(
    facts_width, own_ref, got_ref, gain_ref, squares_ref, facts_ref, kept_ref, sent_ref
):
    width = own_ref.shape[2]
    for chunk, squares in enumerate(norm_part(own_ref, got_ref, gain_ref, kept_ref, sent_ref)):
        facts = facts_ref[...] if chunk == 0 else got_ref[0, :, width:]
        facts = facts.astype(jnp.float32)
        lane = lax.broadcasted_iota(jnp.int32, facts.shape, 1)
        for place, term in enumerate(three_terms(squares + squares_ref[chunk])):
            facts = jnp.where(lane == facts_width + place, term.astype(jnp.float32), facts)
        sent_ref[chunk, :, width:] = facts.astype(jnp.bfloat16)


def normalised(facts_width, own, got, gain, squares=None, facts=None):
    rows, width = own.shape[1:]
    vmem = pl.BlockSpec(memory_space=pltpu.VMEM)
    if squares is None:
        return pl.pallas_call(
            first_norm_kernel,
            out_shape=(
                jax.ShapeDtypeStruct((rows, width), jnp.float32),
                jax.ShapeDtypeStruct((2, rows, width), jnp.bfloat16),
                jax.ShapeDtypeStruct((2, rows, 1), jnp.float32),
            ),
            in_specs=[vmem] * 3,
            out_specs=(vmem,) * 3,
            compiler_params=pltpu.CompilerParams(vmem_limit_bytes=4 << 20),
            name="norm",
        )(own, got, gain[None])
    return pl.pallas_call(
        functools.partial(last_norm_kernel, facts_width),
        out_shape=(
            jax.ShapeDtypeStruct((rows, width), jnp.float32),
            jax.ShapeDtypeStruct((2, rows, width + facts.shape[1]), jnp.bfloat16),
        ),
        in_specs=[vmem] * 5,
        out_specs=(vmem,) * 2,
        compiler_params=pltpu.CompilerParams(vmem_limit_bytes=4 << 20),
        name="norm_last",
    )(own, got, gain[None], squares, facts)


def project_kernel(edge, values_ref, weights_ref, out_ref):
    low, high = edge
    out_ref[...] = jnp.dot(
        values_ref[...], weights_ref[:, low:high], preferred_element_type=jnp.float32
    ).astype(jnp.bfloat16)


def project(values, weights, edge):
    vmem = pl.BlockSpec(memory_space=pltpu.VMEM)
    return pl.pallas_call(
        functools.partial(project_kernel, edge),
        out_shape=jax.ShapeDtypeStruct((values.shape[0], edge[1] - edge[0]), jnp.bfloat16),
        in_specs=[vmem] * 2,
        out_specs=vmem,
        compiler_params=pltpu.CompilerParams(vmem_limit_bytes=8 << 20),
        cost_estimate=pl.CostEstimate(flops=0, bytes_accessed=0, transcendentals=0),
        name="project",
    )(values, weights)


def terms_kernel(edges, hidden_range, *refs):
    row_refs, (gate_ref, up_ref, *more, out_ref) = refs[: len(edges)], refs[len(edges) :]
    start, stop = hidden_range
    for place, weights_ref in enumerate((gate_ref, up_ref)):
        total = 0.0
        for (low, high), row_ref in zip(edges, row_refs):
            total = total + jnp.dot(
                row_ref[...], weights_ref[low:high, start:stop], preferred_element_type=jnp.float32
            )
        width = stop - start
        out_ref[:, place * width : (place + 1) * width] = total.astype(jnp.bfloat16)
    if more:
        placing_ref, facts_ref = more
        out_ref[:, 2 * width :] = jnp.dot(
            placing_ref[...], facts_ref[...], preferred_element_type=jnp.float32
        ).astype(jnp.bfloat16)


def hidden_terms(rows, edges, hidden_range, gate_weights, up_weights, *facts):
    vmem = pl.BlockSpec(memory_space=pltpu.VMEM)
    width = 2 * (hidden_range[1] - hidden_range[0]) + (facts[1].shape[1] if facts else 0)
    return pl.pallas_call(
        functools.partial(terms_kernel, edges, hidden_range),
        out_shape=jax.ShapeDtypeStruct((rows[0].shape[0], width), jnp.bfloat16),
        in_specs=[vmem] * (len(rows) + 2 + len(facts)),
        out_specs=vmem,
        compiler_params=pltpu.CompilerParams(vmem_limit_bytes=8 << 20),
        cost_estimate=pl.CostEstimate(flops=0, bytes_accessed=0, transcendentals=0),
        name="hidden_terms",
    )(*rows, gate_weights, up_weights, *facts)


def three_terms(values):
    first = values.astype(jnp.bfloat16)
    rest = values - first.astype(jnp.float32)
    second = rest.astype(jnp.bfloat16)
    third = (rest - second.astype(jnp.float32)).astype(jnp.bfloat16)
    return first, second, third


def shards(
    queries,
    latent,
    doc_ids,
    w_uv,
    w_out,
    hidden_in,
    norm_gain,
    route_ids,
    route_weights,
    w_gate,
    w_up,
    w_down,
):
    ctx_count = lax.axis_size("ctx")
    ep_count = lax.axis_size("ep")
    ctx_rank = lax.axis_index("ctx")
    ep_rank = lax.axis_index("ep")
    bits = ep_count.bit_length() - 1
    block_rows = queries.shape[0]
    token_count = hidden_in.shape[0]
    top_count = route_ids.shape[1]
    all_tokens = ep_count * token_count
    swap = [(0, 1), (1, 0)]

    key_columns, ctx_rank, ep_rank, lane = lax.optimization_barrier(
        (latent.T, ctx_rank, ep_rank, ep_rank & 1)
    )
    if ctx_count == 2:
        blocks = [key_columns, lax.ppermute(key_columns, "ctx", [(0, 1)])]
    else:
        blocks = [lax.all_gather(key_columns, "ctx", axis=1, tiled=True)]
    head_values = attend(queries, blocks, doc_ids, w_uv)
    route_ids, route_weights, norm_gain, head_values = lax.optimization_barrier(
        (route_ids, route_weights, norm_gain, head_values)
    )

    chunk = jnp.arange(all_tokens, dtype=jnp.int32) // token_count
    owner = chunk_owners(ep_count, ep_rank, lane, chunk)
    if ctx_count == 2:
        other = lax.ppermute(head_values, "ctx", swap)
        w_out = fetched(w_out, head_values)
        all_values = jnp.concatenate([head_values, other], axis=0)
        per_block = ep_count // 2
        owner = owner % per_block + per_block * (owner // per_block != ctx_rank)
    else:
        all_values = lax.all_gather(head_values, "ctx", axis=0, tiled=True)
    row = owner * token_count + jnp.arange(all_tokens, dtype=jnp.int32) % token_count
    ordering = (row[:, None] == jnp.arange(all_tokens, dtype=jnp.int32)[None, :]).astype(
        jnp.bfloat16
    )
    all_values = jnp.dot(ordering, all_values, preferred_element_type=jnp.float32).astype(
        jnp.bfloat16
    )

    experts = jnp.arange(ep_count, dtype=jnp.int32)
    named = route_ids.T[:, :, None] == experts[None, None, :]
    chosen = jnp.sum(named.astype(jnp.float32), axis=0)
    weights = jnp.sum(jnp.where(named, route_weights.T[:, :, None], 0.0), axis=0)
    token_index = jnp.arange(token_count, dtype=jnp.int32)
    before = (token_index[:, None] > token_index[None, :]).astype(jnp.float32)
    place = jnp.sum(before[:, :, None] * chosen[None, :, :], axis=1)
    place = jnp.where(chosen > 0, place, -1.0).astype(jnp.bfloat16)
    facts = jnp.concatenate([place, *three_terms(weights)], axis=1)
    facts_width = facts.shape[1]
    padded = -(-(facts_width + 3) // 128) * 128
    facts = jnp.pad(facts, ((0, 0), (0, padded - facts_width)))

    first_width = w_out.shape[1] // 128 * 15 // 28 * 128
    edges = [(0, first_width), (first_width, w_out.shape[1])]
    residuals, arrived = [], []
    squares = jnp.zeros((2, token_count, 1), jnp.float32)
    for part, (low, high) in enumerate(edges):
        array = project(all_values, w_out, (low, high))
        if part == 0:
            all_values, array = lax.optimization_barrier((all_values, array))
        array = array.reshape(ep_count, token_count, -1)
        for step in range(bits - 1):
            total = halved(array, step, ep_count)
            array = total.astype(jnp.bfloat16)
        own = total[0] + hidden_in[:, low:high].astype(jnp.float32)
        total = jnp.stack([own, total[1]])
        sent = total.astype(jnp.bfloat16)
        last = part == len(edges) - 1
        if last:
            sent = jnp.concatenate([sent, jnp.stack([facts, jnp.zeros_like(facts)])], axis=2)
        got = lax.ppermute(sent, "ep", crossing(ep_count, bits - 1))
        if part == 0:
            gate_weights = fetched(w_gate[0], sent)
            up_weights = fetched(w_up[0], sent)
            got, gate_weights, up_weights = lax.optimization_barrier(
                (got, gate_weights, up_weights)
            )
        width = high - low
        if last:
            kept, array = normalised(facts_width, total, got, norm_gain[low:high], squares, facts)
        else:
            kept, array, more = normalised(facts_width, total, got, norm_gain[low:high])
            squares = squares + more
        residuals.append(kept)
        for step in range(bits - 2, -1, -1):
            array = doubled(array, step, ep_count)
        arrived.append(array.reshape(all_tokens, -1))
    all_facts = arrived[-1][:, width:]
    facts = all_facts.astype(jnp.float32)
    arrived[-1] = arrived[-1][:, :width]

    capacity = min(token_count, max(2, token_count * top_count * 9 // (8 * ep_count)))
    slots = ep_count * capacity
    mine = (experts == ep_rank).astype(jnp.float32)
    of_expert = [
        jnp.sum(facts[:, part * ep_count : (part + 1) * ep_count] * mine[None, :], axis=1)
        for part in range(4)
    ]
    token_place = of_expert[0].astype(jnp.int32)
    token_weight = of_expert[1] + of_expert[2] + of_expert[3]
    token_squares = jnp.sum(facts[:, 4 * ep_count : 4 * ep_count + 3], axis=1)
    token_slot = jnp.where(token_place >= 0, chunk * capacity + token_place, -1)
    placing = jnp.arange(slots, dtype=jnp.int32)[:, None] == token_slot[None, :]
    slot_weight = jnp.sum(jnp.where(placing, token_weight[None, :], 0.0), axis=1)
    placed, placing = placing, placing.astype(jnp.bfloat16)
    rows = [
        jnp.dot(placing, features, preferred_element_type=jnp.float32).astype(jnp.bfloat16)
        for features in arrived
    ]
    hidden = gate_weights.shape[1]
    ranges = split_edges(hidden, HIDDEN_PARTS)
    sums = []
    for hidden_range in ranges:
        beside = (placing, all_facts) if hidden_range is ranges[0] and ctx_count == 2 else ()
        sums.append(hidden_terms(rows, edges, hidden_range, gate_weights, up_weights, *beside))
        if hidden_range is ranges[0]:
            rows[0], sums[0] = lax.optimization_barrier((rows[0], sums[0]))
    if ctx_count == 2:
        others = [lax.ppermute(both, "ctx", swap) for both in sums]
        down_weights = fetched(w_down[0], sums[-1])
        others[0], down_weights = lax.optimization_barrier((others[0], down_weights))
        squares_at = 2 * ranges[0][1] + facts_width
    else:
        down_weights = w_down[0]
        others = [
            lax.psum(both, "ctx").astype(jnp.float32) - both.astype(jnp.float32) for both in sums
        ]
        squares = jnp.where(placed, lax.psum(token_squares, "ctx")[None, :], 0.0)
        slot_squares = jnp.sum(squares, axis=1, keepdims=True)
    out_edges = split_edges(w_out.shape[1], PARTS)
    activated = []
    for place in range(len(ranges)):
        if place == 1:
            others[1], first_products = lax.optimization_barrier((others[1], first_products))
        both = sums[place].astype(jnp.float32) + others[place].astype(jnp.float32)
        if place == 0:
            if ctx_count == 2:
                terms = both[:, squares_at : squares_at + 3]
                slot_squares = jnp.sum(terms, axis=1, keepdims=True)
            slot_scale = lax.rsqrt(slot_squares / D + 1e-06)
        half = ranges[place][1] - ranges[place][0]
        both = both[:, : 2 * half] * slot_scale
        weighted = both[:, half:] * slot_weight[:, None]
        activated.append((jax.nn.silu(both[:, :half]) * weighted).astype(jnp.bfloat16))
        if place == 0:
            start, stop = ranges[0]
            first_products = [
                jnp.dot(
                    activated[0],
                    down_weights[start:stop, low:high],
                    preferred_element_type=jnp.float32,
                )
                for low, high in out_edges
            ]
    spread = placing.T
    outputs = []
    residuals = jnp.concatenate(residuals, axis=1)
    for (low, high), produced in zip(out_edges, first_products):
        residual = residuals[:, low:high]
        for (start, stop), part_rows in zip(ranges[1:], activated[1:]):
            produced = produced + jnp.dot(
                part_rows, down_weights[start:stop, low:high], preferred_element_type=jnp.float32
            )
        produced = produced.astype(jnp.bfloat16)
        produced = lax.optimization_barrier(produced)
        array = (
            jnp.dot(spread, produced, preferred_element_type=jnp.float32)
            .astype(jnp.bfloat16)
            .reshape(ep_count, token_count, -1)
        )
        for step in range(bits):
            total = halved(array, step, ep_count)
            array = total.astype(jnp.bfloat16)
        outputs.append((residual + total[0]).astype(jnp.bfloat16))
    return jnp.concatenate(outputs, axis=1)


def solution(mesh):
    return jax.shard_map(
        shards,
        mesh=mesh,
        in_specs=(
            P("ctx", "ep"),
            P("ctx", None),
            P(),
            P("ep", None, None),
            P("ep", "ctx"),
            P("ep", "ctx"),
            P("ctx"),
            P("ep", None),
            P("ep", None),
            P("ep", "ctx", None),
            P("ep", "ctx", None),
            P("ep", None, "ctx"),
        ),
        out_specs=P("ep", "ctx"),
        check_vma=False,
    )
```

```python
import functools
import math

import jax
import jax.numpy as jnp
from jax import lax
from jax.experimental import pallas as pl
from jax.experimental.pallas import tpu as pltpu
from jax.sharding import PartitionSpec as P

D = 7168
KVL = 512


score_scale = (1.0 + 0.1 * math.log(40.0)) ** 2 / math.sqrt(192.0)
masked_score = -1e30
PARTS = 2
HIDDEN_PARTS = 2


def split_edges(width, parts):
    lanes = width // 128
    edges = [lanes * part // parts * 128 for part in range(parts)] + [width]
    return [(low, high) for low, high in zip(edges[:-1], edges[1:]) if high > low]


def split_columns(array, parts):
    return [array[..., low:high] for low, high in split_edges(array.shape[-1], parts)]


def step_bits(bits, lane):
    middle = list(range(1, bits - 1))
    if not lane:
        middle = middle[1:] + middle[:1]
    return [0] + middle + [bits - 1]


def crossing(count, step):
    bits = count.bit_length() - 1
    return [(index, index ^ (1 << step_bits(bits, index & 1)[step])) for index in range(count)]


def chunk_owners(count, rank, lane, number):
    bits = count.bit_length() - 1
    flip = number >> (bits - 1)
    distances = []
    for side in range(2):
        order = step_bits(bits, side)
        distance = jnp.zeros_like(number)
        for step in range(1, bits):
            distance = distance | ((number >> (bits - 1 - step)) & 1) << order[step]
        distances.append(distance)
    other_lane = (lane ^ flip) == 1
    return rank ^ flip ^ jnp.where(other_lane, distances[1], distances[0])


def halved(array, step, count):
    half = array.shape[0] // 2
    got = lax.ppermute(array[half:], "ep", crossing(count, step))
    return array[:half].astype(jnp.float32) + got.astype(jnp.float32)


def doubled(array, step, count):
    return jnp.concatenate([array, lax.ppermute(array, "ep", crossing(count, step))], axis=0)


def scores_kernel(
    pair_count,
    query_ref,
    keys_ref,
    up_ref,
    doc_ref,
    heads_ref,
    scores_ref,
    own_ref,
    up_out_ref,
    doc_out_ref,
):
    own_ref[...] = keys_ref[...]
    up_out_ref[...] = up_ref[...]
    doc_out_ref[...] = doc_ref[...]
    rows = query_ref.shape[0]
    pair_width = query_ref.shape[1] // pair_count
    width = heads_ref.shape[1]
    half = pair_count * rows
    for side in range(2):
        first = side * (pair_width - width)
        for pair in range(pair_count):
            at = side * half + pair * rows
            low = pair * pair_width + first
            heads_ref[at : at + rows, :] = query_ref[:, low : low + width]
        part = slice(side * half, (side + 1) * half)
        scores_ref[part, :] = jnp.dot(
            heads_ref[part, :], padded_keys(keys_ref, width, side), preferred_element_type=jnp.float32
        )


def padded_keys(keys_ref, width, side):
    zeros = jnp.zeros((width - keys_ref.shape[0], keys_ref.shape[1]), jnp.bfloat16)
    parts = [zeros, keys_ref[...]] if side else [keys_ref[...], zeros]
    return jnp.concatenate(parts, axis=0)


def attend_kernel(pair_count, doc_ref, heads_ref, scores_ref, up_ref, *refs):
    blocks, out_ref = refs[:-1], refs[-1]
    rows = out_ref.shape[0]
    half = pair_count * rows
    width = heads_ref.shape[1]
    value_width = up_ref.shape[2]
    rank = lax.axis_index("ctx")

    def docs_of(first, count):
        return doc_ref[:, pl.ds(pl.multiple_of(first, 128), count)]

    own_first = rank * rows
    query_doc = jnp.broadcast_to(docs_of(own_first, rows), (rows, rows)).T[:, 0:1]
    firsts = [jnp.int32(0)] if len(blocks) == 1 else [own_first, (1 - rank) * rows]
    scores, masks = [], []
    for first, block in zip(firsts, blocks):
        count = block.shape[1]
        key_pos = first + lax.broadcasted_iota(jnp.int32, (rows, count), 1)
        query_pos = own_first + lax.broadcasted_iota(jnp.int32, (rows, count), 0)
        allowed = (key_pos <= query_pos) & (docs_of(first, count) == query_doc)
        masks.append(jnp.where(allowed, 1.0, 0.0))
        if block is blocks[0]:
            scores.append(scores_ref[...])
        else:
            sides = [
                jnp.dot(
                    heads_ref[side * half : (side + 1) * half, :],
                    padded_keys(block, width, side),
                    preferred_element_type=jnp.float32,
                )
                for side in range(2)
            ]
            scores.append(jnp.concatenate(sides, axis=0))
    allowed = jnp.concatenate([jnp.concatenate(masks, axis=1)] * (2 * pair_count), axis=0) > 0
    scores = jnp.where(allowed, jnp.concatenate(scores, axis=1) * score_scale, masked_score)
    peak = jnp.max(scores, axis=1, keepdims=True)
    probs = jnp.where(allowed, jnp.exp(scores - peak), 0.0)
    total = jnp.sum(probs, axis=1, keepdims=True)
    context = lax.dot_general(
        probs.astype(jnp.bfloat16),
        jnp.concatenate([block[:KVL, :] for block in blocks], axis=1),
        (((1,), (1,)), ((), ())),
        preferred_element_type=jnp.float32,
    )
    context = (context / total).astype(jnp.bfloat16)
    for pair in range(pair_count):
        for side in range(2):
            at = side * half + pair * rows
            head = 2 * pair + side
            out_ref[:, head * value_width : (head + 1) * value_width] = jnp.dot(
                context[at : at + rows], up_ref[head], preferred_element_type=jnp.float32
            ).astype(jnp.bfloat16)


def whole_block(shape):
    return pl.BlockSpec(shape, lambda step: (0,) * len(shape))


def in_vmem(grid, spec):
    return spec if grid else pl.BlockSpec(memory_space=pltpu.VMEM)


def attend(queries, blocks, doc_ids, w_uv):
    rows = queries.shape[0]
    head_count, value_in, value_width = w_uv.shape
    query_width = queries.shape[1] // head_count
    key_count = doc_ids.shape[0]
    width = -(-query_width // 128) * 128
    pair_count = head_count // 2 if key_count <= 512 else 1
    heads = 2 * pair_count
    grid = (head_count // heads,) if head_count > heads else ()
    first_keys = blocks[0].shape[1]
    params = pltpu.CompilerParams(
        vmem_limit_bytes=(8 << 20) + 8 * heads * rows * (key_count + KVL) * 4
    )
    stacked = lambda columns: pl.BlockSpec((heads * rows, columns), lambda step: (step, 0))
    up_block = pl.BlockSpec((heads, value_in, value_width), lambda step: (step, 0, 0))
    arranged, scores, own, w_uv, docs = pl.pallas_call(
        functools.partial(scores_kernel, pair_count),
        out_shape=(
            jax.ShapeDtypeStruct((head_count * rows, width), jnp.bfloat16),
            jax.ShapeDtypeStruct((head_count * rows, first_keys), jnp.float32),
            jax.ShapeDtypeStruct(blocks[0].shape, jnp.bfloat16),
            jax.ShapeDtypeStruct(w_uv.shape, jnp.bfloat16),
            jax.ShapeDtypeStruct((1, key_count), jnp.int32),
        ),
        grid=grid,
        in_specs=[
            in_vmem(grid, spec)
            for spec in (
                pl.BlockSpec((rows, heads * query_width), lambda step: (0, step)),
                whole_block(blocks[0].shape),
                up_block,
                whole_block((1, key_count)),
            )
        ],
        out_specs=tuple(
            in_vmem(grid, spec)
            for spec in (
                stacked(width),
                stacked(first_keys),
                whole_block(blocks[0].shape),
                up_block,
                whole_block((1, key_count)),
            )
        ),
        compiler_params=params,
        cost_estimate=pl.CostEstimate(
            flops=2 * rows * head_count * first_keys * width,
            bytes_accessed=2 * queries.size,
            transcendentals=0,
        ),
        name="first_scores",
    )(queries, blocks[0], w_uv, doc_ids[None])
    return pl.pallas_call(
        functools.partial(attend_kernel, pair_count),
        out_shape=jax.ShapeDtypeStruct((rows, head_count * value_width), jnp.bfloat16),
        grid=grid,
        in_specs=[
            in_vmem(grid, spec)
            for spec in (
                whole_block((1, key_count)),
                stacked(width),
                stacked(first_keys),
                up_block,
                *(whole_block(block.shape) for block in blocks),
            )
        ],
        out_specs=in_vmem(
            grid, pl.BlockSpec((rows, heads * value_width), lambda step: (0, step))
        ),
        compiler_params=params,
        cost_estimate=pl.CostEstimate(
            flops=2 * rows * head_count * key_count * (query_width + value_in),
            bytes_accessed=2 * (queries.size + w_uv.size),
            transcendentals=rows * head_count * key_count,
        ),
        name="attention",
    )(docs, arranged, scores, w_uv, own, *blocks[1:])


def fetch_kernel(pieces, first, from_ref, after_ref, to_ref, sems):
    rows = from_ref.shape[0] // pieces
    columns = pl.ds(first, to_ref.shape[1])
    copies = []
    for piece in range(pieces):
        part = pl.ds(piece * rows, rows)
        copies.append(
            pltpu.make_async_copy(
                from_ref.at[part, columns], to_ref.at[part], sems.at[piece]
            )
        )
    for copy in copies:
        copy.start()
    for copy in copies:
        copy.wait()


def fetched(weights, after, edges=None):
    pieces = 4
    low, high = edges or (0, weights.shape[1])
    return pl.pallas_call(
        functools.partial(fetch_kernel, pieces, low),
        out_shape=pltpu.VMEM((weights.shape[0], high - low), weights.dtype),
        in_specs=[
            pl.BlockSpec(memory_space=pltpu.HBM),
            pl.BlockSpec(memory_space=pl.ANY),
        ],
        out_specs=pl.BlockSpec(memory_space=pltpu.VMEM),
        scratch_shapes=[pltpu.SemaphoreType.DMA((pieces,))],
        compiler_params=pltpu.CompilerParams(vmem_limit_bytes=1 << 20),
        cost_estimate=pl.CostEstimate(flops=0, bytes_accessed=0, transcendentals=0),
        name="fetch_weights",
    )(weights, after)


def norm_part(own_ref, got_ref, gain_ref, kept_ref, sent_ref):
    width = own_ref.shape[2]
    squares = []
    for chunk in range(2):
        residual = own_ref[chunk] + got_ref[1 - chunk, :, :width].astype(jnp.float32)
        if chunk == 0:
            kept_ref[...] = residual
        sent_ref[chunk, :, :width] = (residual * gain_ref[...]).astype(jnp.bfloat16)
        squares.append(jnp.sum(residual * residual, axis=1, keepdims=True))
    return squares


def first_norm_kernel(own_ref, got_ref, gain_ref, kept_ref, sent_ref, squares_ref):
    for chunk, squares in enumerate(norm_part(own_ref, got_ref, gain_ref, kept_ref, sent_ref)):
        squares_ref[chunk] = squares


def last_norm_kernel(
    facts_width, own_ref, got_ref, gain_ref, squares_ref, facts_ref, kept_ref, sent_ref
):
    width = own_ref.shape[2]
    for chunk, squares in enumerate(norm_part(own_ref, got_ref, gain_ref, kept_ref, sent_ref)):
        facts = facts_ref[...] if chunk == 0 else got_ref[0, :, width:]
        facts = facts.astype(jnp.float32)
        lane = lax.broadcasted_iota(jnp.int32, facts.shape, 1)
        for place, term in enumerate(three_terms(squares + squares_ref[chunk])):
            facts = jnp.where(lane == facts_width + place, term.astype(jnp.float32), facts)
        sent_ref[chunk, :, width:] = facts.astype(jnp.bfloat16)


def normalised(facts_width, own, got, gain, squares=None, facts=None):
    rows, width = own.shape[1:]
    vmem = pl.BlockSpec(memory_space=pltpu.VMEM)
    if squares is None:
        return pl.pallas_call(
            first_norm_kernel,
            out_shape=(
                jax.ShapeDtypeStruct((rows, width), jnp.float32),
                jax.ShapeDtypeStruct((2, rows, width), jnp.bfloat16),
                jax.ShapeDtypeStruct((2, rows, 1), jnp.float32),
            ),
            in_specs=[vmem] * 3,
            out_specs=(vmem,) * 3,
            compiler_params=pltpu.CompilerParams(vmem_limit_bytes=4 << 20),
            name="norm",
        )(own, got, gain[None])
    return pl.pallas_call(
        functools.partial(last_norm_kernel, facts_width),
        out_shape=(
            jax.ShapeDtypeStruct((rows, width), jnp.float32),
            jax.ShapeDtypeStruct((2, rows, width + facts.shape[1]), jnp.bfloat16),
        ),
        in_specs=[vmem] * 5,
        out_specs=(vmem,) * 2,
        compiler_params=pltpu.CompilerParams(vmem_limit_bytes=4 << 20),
        name="norm_last",
    )(own, got, gain[None], squares, facts)


def project_kernel(edge, values_ref, weights_ref, out_ref):
    low, high = edge
    out_ref[...] = jnp.dot(
        values_ref[...], weights_ref[:, low:high], preferred_element_type=jnp.float32
    ).astype(jnp.bfloat16)


def project(values, weights, edge):
    vmem = pl.BlockSpec(memory_space=pltpu.VMEM)
    return pl.pallas_call(
        functools.partial(project_kernel, edge),
        out_shape=jax.ShapeDtypeStruct((values.shape[0], edge[1] - edge[0]), jnp.bfloat16),
        in_specs=[vmem] * 2,
        out_specs=vmem,
        compiler_params=pltpu.CompilerParams(vmem_limit_bytes=8 << 20),
        cost_estimate=pl.CostEstimate(flops=0, bytes_accessed=0, transcendentals=0),
        name="project",
    )(values, weights)


def output_kernel(edges, out_edges, *refs):
    out_ref = refs[-1]
    residual_refs, sums = refs[: len(edges)], refs[len(edges) : -1]
    for place, (start, stop) in enumerate(out_edges):
        kept_ref, got_ref = sums[2 * place], sums[2 * place + 1]
        for (low, high), residual_ref in zip(edges, residual_refs):
            first, last = max(low, start), min(high, stop)
            if first < last:
                own, at = slice(first - low, last - low), slice(first - start, last - start)
                total = kept_ref[0, :, at].astype(jnp.float32) + got_ref[0, :, at].astype(jnp.float32)
                out_ref[:, first:last] = (residual_ref[:, own] + total).astype(jnp.bfloat16)


def terms_kernel(edges, hidden_range, *refs):
    row_refs, (gate_ref, up_ref, *more, out_ref) = refs[: len(edges)], refs[len(edges) :]
    start, stop = hidden_range
    for place, weights_ref in enumerate((gate_ref, up_ref)):
        total = 0.0
        for (low, high), row_ref in zip(edges, row_refs):
            total = total + jnp.dot(
                row_ref[...], weights_ref[low:high, start:stop], preferred_element_type=jnp.float32
            )
        width = stop - start
        out_ref[:, place * width : (place + 1) * width] = total.astype(jnp.bfloat16)
    if more:
        placing_ref, facts_ref = more
        out_ref[:, 2 * width :] = jnp.dot(
            placing_ref[...], facts_ref[...], preferred_element_type=jnp.float32
        ).astype(jnp.bfloat16)


def hidden_terms(rows, edges, hidden_range, gate_weights, up_weights, *facts):
    vmem = pl.BlockSpec(memory_space=pltpu.VMEM)
    width = 2 * (hidden_range[1] - hidden_range[0]) + (facts[1].shape[1] if facts else 0)
    return pl.pallas_call(
        functools.partial(terms_kernel, edges, hidden_range),
        out_shape=jax.ShapeDtypeStruct((rows[0].shape[0], width), jnp.bfloat16),
        in_specs=[vmem] * (len(rows) + 2 + len(facts)),
        out_specs=vmem,
        compiler_params=pltpu.CompilerParams(vmem_limit_bytes=8 << 20),
        cost_estimate=pl.CostEstimate(flops=0, bytes_accessed=0, transcendentals=0),
        name="hidden_terms",
    )(*rows, gate_weights, up_weights, *facts)


def three_terms(values):
    first = values.astype(jnp.bfloat16)
    rest = values - first.astype(jnp.float32)
    second = rest.astype(jnp.bfloat16)
    third = (rest - second.astype(jnp.float32)).astype(jnp.bfloat16)
    return first, second, third


def shards(
    queries,
    latent,
    doc_ids,
    w_uv,
    w_out,
    hidden_in,
    norm_gain,
    route_ids,
    route_weights,
    w_gate,
    w_up,
    w_down,
):
    ctx_count = lax.axis_size("ctx")
    ep_count = lax.axis_size("ep")
    ctx_rank = lax.axis_index("ctx")
    ep_rank = lax.axis_index("ep")
    bits = ep_count.bit_length() - 1
    block_rows = queries.shape[0]
    token_count = hidden_in.shape[0]
    top_count = route_ids.shape[1]
    all_tokens = ep_count * token_count
    swap = [(0, 1), (1, 0)]

    key_columns, ctx_rank, ep_rank, lane = lax.optimization_barrier(
        (latent.T, ctx_rank, ep_rank, ep_rank & 1)
    )
    if ctx_count == 2:
        blocks = [key_columns, lax.ppermute(key_columns, "ctx", [(0, 1)])]
    else:
        blocks = [lax.all_gather(key_columns, "ctx", axis=1, tiled=True)]
    head_values = attend(queries, blocks, doc_ids, w_uv)
    route_ids, route_weights, norm_gain, head_values = lax.optimization_barrier(
        (route_ids, route_weights, norm_gain, head_values)
    )

    chunk = jnp.arange(all_tokens, dtype=jnp.int32) // token_count
    owner = chunk_owners(ep_count, ep_rank, lane, chunk)
    if ctx_count == 2:
        other = lax.ppermute(head_values, "ctx", swap)
        w_out = fetched(w_out, head_values)
        all_values = jnp.concatenate([head_values, other], axis=0)
        per_block = ep_count // 2
        owner = owner % per_block + per_block * (owner // per_block != ctx_rank)
    else:
        all_values = lax.all_gather(head_values, "ctx", axis=0, tiled=True)
    row = owner * token_count + jnp.arange(all_tokens, dtype=jnp.int32) % token_count
    ordering = (row[:, None] == jnp.arange(all_tokens, dtype=jnp.int32)[None, :]).astype(
        jnp.bfloat16
    )
    all_values = jnp.dot(ordering, all_values, preferred_element_type=jnp.float32).astype(
        jnp.bfloat16
    )

    experts = jnp.arange(ep_count, dtype=jnp.int32)
    named = route_ids.T[:, :, None] == experts[None, None, :]
    chosen = jnp.sum(named.astype(jnp.float32), axis=0)
    weights = jnp.sum(jnp.where(named, route_weights.T[:, :, None], 0.0), axis=0)
    token_index = jnp.arange(token_count, dtype=jnp.int32)
    before = (token_index[:, None] > token_index[None, :]).astype(jnp.float32)
    place = jnp.sum(before[:, :, None] * chosen[None, :, :], axis=1)
    place = jnp.where(chosen > 0, place, -1.0).astype(jnp.bfloat16)
    facts = jnp.concatenate([place, *three_terms(weights)], axis=1)
    facts_width = facts.shape[1]
    padded = -(-(facts_width + 3) // 128) * 128
    facts = jnp.pad(facts, ((0, 0), (0, padded - facts_width)))

    first_width = w_out.shape[1] // 128 * 15 // 28 * 128
    edges = [(0, first_width), (first_width, w_out.shape[1])]
    residuals, arrived = [], []
    squares = jnp.zeros((2, token_count, 1), jnp.float32)
    for part, (low, high) in enumerate(edges):
        array = project(all_values, w_out, (low, high))
        if part == 0:
            all_values, array = lax.optimization_barrier((all_values, array))
        array = array.reshape(ep_count, token_count, -1)
        for step in range(bits - 1):
            total = halved(array, step, ep_count)
            array = total.astype(jnp.bfloat16)
        own = total[0] + hidden_in[:, low:high].astype(jnp.float32)
        total = jnp.stack([own, total[1]])
        sent = total.astype(jnp.bfloat16)
        last = part == len(edges) - 1
        if last:
            sent = jnp.concatenate([sent, jnp.stack([facts, jnp.zeros_like(facts)])], axis=2)
        got = lax.ppermute(sent, "ep", crossing(ep_count, bits - 1))
        if part == 0:
            gate_weights = fetched(w_gate[0], sent)
            up_weights = fetched(w_up[0], sent)
            got, gate_weights, up_weights = lax.optimization_barrier(
                (got, gate_weights, up_weights)
            )
        width = high - low
        if last:
            kept, array = normalised(facts_width, total, got, norm_gain[low:high], squares, facts)
        else:
            kept, array, more = normalised(facts_width, total, got, norm_gain[low:high])
            squares = squares + more
        residuals.append(kept)
        for step in range(bits - 2, -1, -1):
            array = doubled(array, step, ep_count)
        arrived.append(array.reshape(all_tokens, -1))
    all_facts = arrived[-1][:, width:]
    facts = all_facts.astype(jnp.float32)
    arrived[-1] = arrived[-1][:, :width]

    capacity = min(token_count, max(2, token_count * top_count * 9 // (8 * ep_count)))
    slots = ep_count * capacity
    mine = (experts == ep_rank).astype(jnp.float32)
    of_expert = [
        jnp.sum(facts[:, part * ep_count : (part + 1) * ep_count] * mine[None, :], axis=1)
        for part in range(4)
    ]
    token_place = of_expert[0].astype(jnp.int32)
    token_weight = of_expert[1] + of_expert[2] + of_expert[3]
    token_squares = jnp.sum(facts[:, 4 * ep_count : 4 * ep_count + 3], axis=1)
    token_slot = jnp.where(token_place >= 0, chunk * capacity + token_place, -1)
    placing = jnp.arange(slots, dtype=jnp.int32)[:, None] == token_slot[None, :]
    slot_weight = jnp.sum(jnp.where(placing, token_weight[None, :], 0.0), axis=1)
    placed, placing = placing, placing.astype(jnp.bfloat16)
    rows = [
        jnp.dot(placing, features, preferred_element_type=jnp.float32).astype(jnp.bfloat16)
        for features in arrived
    ]
    hidden = gate_weights.shape[1]
    ranges = split_edges(hidden, HIDDEN_PARTS)
    sums = []
    for hidden_range in ranges:
        beside = (placing, all_facts) if hidden_range is ranges[0] and ctx_count == 2 else ()
        sums.append(hidden_terms(rows, edges, hidden_range, gate_weights, up_weights, *beside))
        if hidden_range is ranges[0]:
            rows[0], sums[0] = lax.optimization_barrier((rows[0], sums[0]))
    if ctx_count == 2:
        others = [lax.ppermute(both, "ctx", swap) for both in sums]
        down_weights = fetched(w_down[0], sums[-1])
        others[0], down_weights = lax.optimization_barrier((others[0], down_weights))
        squares_at = 2 * ranges[0][1] + facts_width
    else:
        down_weights = w_down[0]
        others = [
            lax.psum(both, "ctx").astype(jnp.float32) - both.astype(jnp.float32) for both in sums
        ]
        squares = jnp.where(placed, lax.psum(token_squares, "ctx")[None, :], 0.0)
        slot_squares = jnp.sum(squares, axis=1, keepdims=True)
    out_edges = split_edges(w_out.shape[1], PARTS)
    activated = []
    for place in range(len(ranges)):
        if place == 1:
            others[1], first_products = lax.optimization_barrier((others[1], first_products))
        both = sums[place].astype(jnp.float32) + others[place].astype(jnp.float32)
        if place == 0:
            if ctx_count == 2:
                terms = both[:, squares_at : squares_at + 3]
                slot_squares = jnp.sum(terms, axis=1, keepdims=True)
            slot_scale = lax.rsqrt(slot_squares / D + 1e-06)
        half = ranges[place][1] - ranges[place][0]
        both = both[:, : 2 * half] * slot_scale
        weighted = both[:, half:] * slot_weight[:, None]
        activated.append((jax.nn.silu(both[:, :half]) * weighted).astype(jnp.bfloat16))
        if place == 0:
            start, stop = ranges[0]
            first_products = [
                jnp.dot(
                    activated[0],
                    down_weights[start:stop, low:high],
                    preferred_element_type=jnp.float32,
                )
                for low, high in out_edges
            ]
    spread = placing.T
    outputs = []
    for (low, high), produced in zip(out_edges, first_products):
        for (start, stop), part_rows in zip(ranges[1:], activated[1:]):
            produced = produced + jnp.dot(
                part_rows, down_weights[start:stop, low:high], preferred_element_type=jnp.float32
            )
        produced = produced.astype(jnp.bfloat16)
        produced = lax.optimization_barrier(produced)
        array = (
            jnp.dot(spread, produced, preferred_element_type=jnp.float32)
            .astype(jnp.bfloat16)
            .reshape(ep_count, token_count, -1)
        )
        for step in range(bits - 1):
            array = halved(array, step, ep_count).astype(jnp.bfloat16)
        got = lax.ppermute(array[1:], "ep", crossing(ep_count, bits - 1))
        outputs.extend([array[:1], got])
    vmem = pl.BlockSpec(memory_space=pltpu.VMEM)
    return pl.pallas_call(
        functools.partial(output_kernel, edges, out_edges),
        out_shape=jax.ShapeDtypeStruct(hidden_in.shape, jnp.bfloat16),
        in_specs=[vmem] * (len(residuals) + len(outputs)),
        out_specs=vmem,
        compiler_params=pltpu.CompilerParams(vmem_limit_bytes=4 << 20),
        name="output",
    )(*residuals, *outputs)


def solution(mesh):
    return jax.shard_map(
        shards,
        mesh=mesh,
        in_specs=(
            P("ctx", "ep"),
            P("ctx", None),
            P(),
            P("ep", None, None),
            P("ep", "ctx"),
            P("ep", "ctx"),
            P("ctx"),
            P("ep", None),
            P("ep", None),
            P("ep", "ctx", None),
            P("ep", "ctx", None),
            P("ep", None, "ctx"),
        ),
        out_specs=P("ep", "ctx"),
        check_vma=False,
    )
```
